256 devices in a mesh: blk: 32 (over y_lo, z, core), head: 8 (over x, y_hi).
Axes of the slice: x: 4, y: 4 (y_hi: 2, y_lo: 2; y = y_hi * 2 + y_lo), z: 8, core: 2. Of those that a mesh axis runs over, the one named last changes fastest.
Arguments:
- queries: bfloat16 [2048, 128, 128], P('blk', 'head'), may hold values from -6 to 6
- unrotated_key_rows: bfloat16 [2048, 8, 128], P('blk', 'head'), may hold values from -6 to 6
- incoming_value_rows: bfloat16 [2048, 8, 128], P('blk', 'head'), may hold values from -6 to 6
- cache_keys: bfloat16 [32, 16, 8, 256, 128], P('blk', None, 'head'), may hold values from -135 to 135
- stored_value_rows: bfloat16 [32, 16, 8, 256, 128], P('blk', None, 'head'), may hold values from -6 to 6
- cache_len: int32 [32, 16], P('blk'), may hold values from 32 to 256, as said below
- new_count: int32 [16], replicated, may hold values from 1 to 128, 1280 in all
- slot_index: int32 [32, 16, 4], replicated, may hold values from 0 to 127, as said below
- out_weight: bfloat16 [16384, 16384], P('head', 'blk'), may hold values from -0.5 to 0.5
Outputs:
- projected: bfloat16 [2048, 16384], P('head', 'blk')
The draws below stay inside these ranges and needn't reach their ends.
Inputs may be any that keep to these rules, and one draw needn't show every extreme that they name: `slot_index`: for every conversation each index from 0 to 127 stands in exactly one slot. `cache_len`: in every conversation some shard is full.
All inputs are finite; a program needn't handle non-finite values.
Results may differ from the reference program's by a relative error of at most 0.019.
Values may be sent and summed in bfloat16 or wider, within the bound.
No kernel may reach another device: no remote copies, remote signals or barrier semaphores. Data moves between devices by JAX's collectives and lax.ppermute only.
A program may use at most 128 MiB of HBM per device.

```python
import math
import jax
import jax.numpy as jnp
import numpy as np
from jax import lax

D = 16384
QUERY_HEADS = 128
KEY_VALUE_HEADS = 8
HEAD_SIZE = 128
CONVERSE_COUNT = 16
DEVICE_NEW_SLOTS = 4
DEVICE_CACHE_SLOT = 256
NEW_SLOT_LIMIT = 128
NEW_TOKENS = 1280
TOTAL_NEW_ROWS = 2048
N_BLK = 32


def draw_slot_index(key, part):
    key = jax.random.fold_in(key, 11)
    shard_count = NEW_SLOT_LIMIT // DEVICE_NEW_SLOTS

    def one_list(conversation_number):
        return jax.random.permutation(jax.random.fold_in(key, conversation_number), NEW_SLOT_LIMIT)
    lists = jax.vmap(one_list)(jnp.arange(CONVERSE_COUNT, dtype=jnp.int32))
    return jnp.transpose(lists.reshape(CONVERSE_COUNT, shard_count, DEVICE_NEW_SLOTS), (1, 0, 2)).astype(jnp.int32)


def draw_cache_len(key, part):
    key = jax.random.fold_in(key, 12)
    shard_count = NEW_SLOT_LIMIT // DEVICE_NEW_SLOTS
    first_key, second_key = jax.random.split(key)
    lengths = jax.random.randint(first_key, (shard_count, CONVERSE_COUNT), DEVICE_CACHE_SLOT // 8, DEVICE_CACHE_SLOT + 1)
    full_shard = jax.random.randint(second_key, (CONVERSE_COUNT,), 0, shard_count)
    lengths = jnp.where(jnp.arange(shard_count)[:, None] == full_shard[None, :], DEVICE_CACHE_SLOT, lengths)
    return lengths.astype(jnp.int32)


def draw_cache_keys(key, part):
    key = jax.random.fold_in(key, 13)
    array_dimensions = (NEW_SLOT_LIMIT // DEVICE_NEW_SLOTS, CONVERSE_COUNT, KEY_VALUE_HEADS, DEVICE_CACHE_SLOT, HEAD_SIZE)
    first_key = jax.random.fold_in(key, 0)
    return (1.3 * jnp.clip(jax.random.normal(first_key, array_dimensions, jnp.float32), -6.0, 6.0)).astype(jnp.bfloat16)


def shard_levels(rng, extent, cuts, low, largest):
    gain, own = 1.0, jax.random.fold_in(rng, 6)
    for dim, blocks in cuts:
        heights = jnp.exp(jax.random.uniform(jax.random.fold_in(own, dim), (blocks,), jnp.float32, low / len(cuts), largest / len(cuts)))
        gain = gain * jnp.repeat(heights, extent[dim] // blocks).reshape([-1 if axis == dim else 1 for axis in range(len(extent))])
    return gain


def split_up(count, total, bound, skew):
    weights = [(1 << 20) // math.isqrt(standing ** skew) + 1 for standing in range(2, count + 1)]
    spare, counts = total - bound - (count - 1), [1] * (count - 1)
    while spare > 0:
        free = [i for i in range(count - 1) if counts[i] < bound]
        mass, budget = sum([weights[i] for i in free]), spare
        for i in free:
            addition = min(bound - counts[i], max(1, budget * weights[i] // mass), spare)
            counts[i] = counts[i] + addition
            spare = spare - addition
    return np.array([bound] + counts)


def ragged_sizes(stream_key, number_of, total, reach, lean):
    if number_of == 2:
        one = jax.random.randint(stream_key, (), max(1, total - reach), min(reach, total - 1) + 1)
        return jnp.stack([one, total - one])
    sizes = jnp.asarray(split_up(number_of, total, reach, lean), jnp.int32)
    couples = (number_of - 1) // 2
    source_of, receiver = sizes[1:1 + 2 * couples:2], sizes[2:2 + 2 * couples:2]
    room = jnp.minimum(source_of - 1, reach - receiver)
    shifted = jax.random.randint(jax.random.fold_in(stream_key, 1), (couples,), 0, 1 << 20) % (room + 1)
    sizes = sizes.at[1:1 + 2 * couples:2].set(source_of - shifted).at[2:2 + 2 * couples:2].set(receiver + shifted)
    return sizes[jax.random.permutation(jax.random.fold_in(stream_key, 2), number_of)]


def normal_values(stream_key, shape, width, reach, shards=(), kind=jnp.bfloat16):
    values = jax.random.normal(stream_key, shape, jnp.float32) * width
    if len(shards) > 0:
        values = shard_levels(stream_key, shape, shards, -0.22, 0.18) * values
    return jnp.clip(values, min=-reach, max=reach).astype(kind)


def setup_inputs(seed: int = 0) -> dict:
    seeds = jax.random.split(jax.random.key(seed), 10)
    queries = normal_values(seeds[0], (TOTAL_NEW_ROWS, QUERY_HEADS, HEAD_SIZE), 1.5, 6.0, ((0, 32), (1, 8)))
    unrotated_key_rows = normal_values(seeds[1], (TOTAL_NEW_ROWS, KEY_VALUE_HEADS, HEAD_SIZE), 1.3, 6.0, ((0, 32), (1, 8)))
    incoming_value_rows = normal_values(seeds[2], (TOTAL_NEW_ROWS, KEY_VALUE_HEADS, HEAD_SIZE), 1.0, 6.0, ((0, 32), (1, 8)))
    cache_keys = draw_cache_keys(jax.random.fold_in(seeds[9], 71), 0)
    stored_value_rows = normal_values(seeds[4], (N_BLK, CONVERSE_COUNT, KEY_VALUE_HEADS, DEVICE_CACHE_SLOT, HEAD_SIZE), 1.0, 6.0, ((0, 32), (2, 8)))
    cache_len = draw_cache_len(jax.random.fold_in(seeds[9], 71), 0)
    new_count = ragged_sizes(seeds[6], CONVERSE_COUNT, NEW_TOKENS, NEW_SLOT_LIMIT, 2).astype(jnp.int32)
    slot_index = draw_slot_index(jax.random.fold_in(seeds[9], 71), 0)
    out_weight = normal_values(seeds[8], (QUERY_HEADS * HEAD_SIZE, D), HEAD_SIZE ** -0.5, 0.5, ((0, 8), (1, 32)))
    return dict(queries=queries, unrotated_key_rows=unrotated_key_rows, incoming_value_rows=incoming_value_rows, cache_keys=cache_keys, stored_value_rows=stored_value_rows, cache_len=cache_len, new_count=new_count, slot_index=slot_index, out_weight=out_weight)


def rotate(values, positions):
    half_width = values.shape[-1] // 2
    inverse = 1.0 / (500000.0 ** (jnp.arange(0, values.shape[-1], 2, dtype=jnp.float32) / values.shape[-1]))
    angles = positions[..., None] * inverse
    cosine = jnp.cos(angles)
    sine_part = jnp.sin(angles)
    first_half = values[..., :half_width]
    second_half = values[..., half_width:]
    return jnp.concatenate([first_half * cosine - second_half * sine_part, second_half * cosine + first_half * sine_part], -1)


def reference(queries, unrotated_key_rows, incoming_value_rows, cache_keys, stored_value_rows, cache_len, new_count, slot_index, out_weight):
    query_group_width = QUERY_HEADS // KEY_VALUE_HEADS
    slot_row_indices = N_BLK * DEVICE_NEW_SLOTS
    scaling = HEAD_SIZE ** -0.5
    cache_totals = jnp.sum(cache_len, axis=0).astype(jnp.float32)
    queries_all = queries.reshape(N_BLK, CONVERSE_COUNT, DEVICE_NEW_SLOTS, QUERY_HEADS, HEAD_SIZE)
    joined_key_rows = unrotated_key_rows.reshape(N_BLK, CONVERSE_COUNT, DEVICE_NEW_SLOTS, KEY_VALUE_HEADS, HEAD_SIZE)
    joined_value_rows = incoming_value_rows.reshape(N_BLK, CONVERSE_COUNT, DEVICE_NEW_SLOTS, KEY_VALUE_HEADS, HEAD_SIZE)

    def one_conversation(conversation_number):
        conv_queries = lax.dynamic_index_in_dim(queries_all, conversation_number, 1, keepdims=False).reshape(slot_row_indices, QUERY_HEADS, HEAD_SIZE)
        conversation_key_rows = lax.dynamic_index_in_dim(joined_key_rows, conversation_number, 1, keepdims=False).reshape(slot_row_indices, KEY_VALUE_HEADS, HEAD_SIZE)
        conversation_value_rows = lax.dynamic_index_in_dim(joined_value_rows, conversation_number, 1, keepdims=False).reshape(slot_row_indices, KEY_VALUE_HEADS, HEAD_SIZE)
        token_index = lax.dynamic_index_in_dim(slot_index, conversation_number, 1, keepdims=False).reshape(slot_row_indices)
        token_count = new_count[conversation_number]
        positions = cache_totals[conversation_number] + token_index.astype(jnp.float32)
        queries_rot = rotate(conv_queries.astype(jnp.float32), positions[:, None]).astype(jnp.bfloat16)
        keys_rot = rotate(conversation_key_rows.astype(jnp.float32), positions[:, None]).astype(jnp.bfloat16)
        shard_lengths = lax.dynamic_index_in_dim(cache_len, conversation_number, 1, keepdims=False)
        cache_allowed = (jnp.arange(DEVICE_CACHE_SLOT)[None, :] < shard_lengths[:, None]).reshape(N_BLK * DEVICE_CACHE_SLOT)
        new_allowed = (token_index[None, :] < token_count) & (token_index[None, :] <= token_index[:, None])
        query_live = token_index < token_count
        conv_cache_keys = lax.dynamic_index_in_dim(cache_keys, conversation_number, 1, keepdims=False)
        conv_cache_values = lax.dynamic_index_in_dim(stored_value_rows, conversation_number, 1, keepdims=False)

        def single_head_output(head_id):
            head_queries = lax.dynamic_slice_in_dim(queries_rot, head_id * query_group_width, query_group_width, 1)
            flat_queries = head_queries.reshape(slot_row_indices * query_group_width, HEAD_SIZE)
            keys_cache = lax.dynamic_index_in_dim(conv_cache_keys, head_id, 1, keepdims=False).reshape(N_BLK * DEVICE_CACHE_SLOT, HEAD_SIZE)
            values_cache = lax.dynamic_index_in_dim(conv_cache_values, head_id, 1, keepdims=False).reshape(N_BLK * DEVICE_CACHE_SLOT, HEAD_SIZE)
            keys_new = lax.dynamic_index_in_dim(keys_rot, head_id, 1, keepdims=False)
            values_new = lax.dynamic_index_in_dim(conversation_value_rows, head_id, 1, keepdims=False)
            cache_scores = jnp.dot(flat_queries, keys_cache.T, preferred_element_type=jnp.float32) * scaling
            cache_scores = cache_scores.reshape(slot_row_indices, query_group_width, N_BLK * DEVICE_CACHE_SLOT)
            new_scores = jnp.dot(flat_queries, keys_new.T, preferred_element_type=jnp.float32) * scaling
            new_scores = new_scores.reshape(slot_row_indices, query_group_width, slot_row_indices)
            cache_scores = jnp.where(cache_allowed[None, None, :], cache_scores, -jnp.inf)
            new_scores = jnp.where(new_allowed[:, None, :], new_scores, -jnp.inf)
            highest = jnp.maximum(jnp.max(cache_scores, -1), jnp.max(new_scores, -1))
            cache_weights = jnp.exp(cache_scores - highest[..., None])
            new_weights = jnp.exp(new_scores - highest[..., None])
            denominator = jnp.sum(cache_weights, -1) + jnp.sum(new_weights, -1)
            numerator = jnp.dot(cache_weights.astype(jnp.bfloat16).reshape(slot_row_indices * query_group_width, N_BLK * DEVICE_CACHE_SLOT), values_cache, preferred_element_type=jnp.float32)
            numerator = numerator + jnp.dot(new_weights.astype(jnp.bfloat16).reshape(slot_row_indices * query_group_width, slot_row_indices), values_new, preferred_element_type=jnp.float32)
            result = numerator.reshape(slot_row_indices, query_group_width, HEAD_SIZE) / denominator[..., None]
            return jnp.where(query_live[:, None, None], result, 0.0)

        head_output_rows = lax.map(single_head_output, jnp.arange(KEY_VALUE_HEADS, dtype=jnp.int32))
        return jnp.transpose(head_output_rows, (1, 0, 2, 3)).reshape(slot_row_indices, QUERY_HEADS, HEAD_SIZE)

    outputs = lax.map(one_conversation, jnp.arange(CONVERSE_COUNT, dtype=jnp.int32))
    outputs = outputs.reshape(CONVERSE_COUNT, N_BLK, DEVICE_NEW_SLOTS, QUERY_HEADS * HEAD_SIZE)
    attended = jnp.transpose(outputs, (1, 0, 2, 3)).reshape(TOTAL_NEW_ROWS, QUERY_HEADS * HEAD_SIZE).astype(jnp.bfloat16)
    return jnp.dot(attended, out_weight, preferred_element_type=jnp.float32).astype(jnp.bfloat16)
```

```python
import functools

import jax
import jax.numpy as jnp
from jax import lax
from jax.experimental import pallas as pl
from jax.experimental.pallas import tpu as pltpu
from jax.sharding import Mesh, PartitionSpec as P

LOG2_E = 1.4426950408889634
ROWS = 256
CLOSED = 1.0e9
LEGS = (
    ((1, 0), (0, 1), (0, -1)),
    ((1, 1), (1, -1), (0, 2), (0, -2)),
    ((1, 2), (1, -2), (0, 3), (0, -3)),
    ((1, 3), (1, -3), (0, 4), (1, 4)),
)


def attend_kernel(shards, first, last, lens_ref, q_ref, *refs):
    refs = list(refs)
    shard_refs = [refs.pop(0) for _ in range(shards)]
    if first:
        new_k_ref, new_v_ref, key_index_ref, row_index_ref = [refs.pop(0) for _ in range(4)]
    else:
        sums_in, stats_in = [refs.pop(0) for _ in range(2)]
    sums_out, stats_out = [refs.pop(0) for _ in range(2)]
    q = q_ref[0]
    scale = LOG2_E / q.shape[-1] ** 0.5
    slots = shard_refs[0].shape[0] // 2
    slot = lax.broadcasted_iota(jnp.int32, (slots, 1), 0)
    scores, values = [], []
    for i, ref in enumerate(shard_refs):
        s = lax.dot_general(
            ref[0:slots, :], q, (((1,), (1,)), ((), ())), preferred_element_type=jnp.float32
        )
        scores.append(jnp.where(slot < lens_ref[i], s * scale, -jnp.inf))
        values.append(ref[slots : 2 * slots, :])
    if first:
        s = lax.dot_general(
            new_k_ref[...], q, (((1,), (1,)), ((), ())), preferred_element_type=jnp.float32
        )
        seen = key_index_ref[:, 0:1] <= row_index_ref[0, 0:1, :]
        scores.append(jnp.where(seen, s * scale, -jnp.inf))
        values.append(new_v_ref[...])
    top = functools.reduce(jnp.maximum, [jnp.max(s, axis=0, keepdims=True) for s in scores])
    if first:
        total = jnp.zeros_like(top)
        sums = jnp.zeros((q.shape[-1], q.shape[0]), jnp.float32)
    else:
        before = stats_in[0, 0:1, :]
        top = jnp.maximum(top, before)
        shrink = jnp.exp2(before - top)
        total = stats_in[0, 1:2, :] * shrink
        sums = sums_in[0] * shrink
    for s, v in zip(scores, values):
        w = jnp.exp2(s - top)
        total = total + jnp.sum(w, axis=0, keepdims=True)
        sums = sums + lax.dot_general(
            v, w.astype(jnp.bfloat16), (((0,), (0,)), ((), ())), preferred_element_type=jnp.float32
        )
    sums_out[0] = sums
    stats_out[0] = jnp.concatenate([top, total, jnp.zeros((6, q.shape[0]), jnp.float32)], 0)
    if last:
        message = refs.pop(0)
        width = q.shape[-1]
        message[0, 0:width, :] = sums.astype(jnp.bfloat16)
        rows = []
        for value in (top, total):
            for _ in range(3):
                part = value.astype(jnp.bfloat16).astype(jnp.float32)
                rows.append(part)
                value = value - part
        rows.append(jnp.zeros((10, q.shape[0]), jnp.float32))
        message[0, width : width + 16, :] = jnp.concatenate(rows, 0).astype(jnp.bfloat16)


def attend(lens, q, shards, state, new, last):
    halves, rows, width = q.shape
    whole = lambda a: pl.BlockSpec(a.shape, lambda i, j: (0,) * a.ndim)
    lanes = lambda depth: pl.BlockSpec((1, depth, ROWS), lambda i, j: (i, 0, j))
    in_specs = [
        pl.BlockSpec(memory_space=pltpu.SMEM),
        pl.BlockSpec((1, ROWS, width), lambda i, j: (i, j, 0)),
    ]
    in_specs += [whole(a) for a in shards]
    if state is None:
        in_specs += [whole(a) for a in new[:3]] + [lanes(8)]
        extra = tuple(new)
    else:
        in_specs += [lanes(width), lanes(8)]
        extra = tuple(state)
    out_shape = [
        jax.ShapeDtypeStruct((halves, width, rows), jnp.float32),
        jax.ShapeDtypeStruct((halves, 8, rows), jnp.float32),
    ]
    out_specs = [lanes(width), lanes(8)]
    if last:
        out_shape.append(jax.ShapeDtypeStruct((halves, width + 16, rows), jnp.bfloat16))
        out_specs.append(lanes(width + 16))
    keys = sum(a.shape[0] // 2 for a in shards)
    return pl.pallas_call(
        functools.partial(attend_kernel, len(shards), state is None, last),
        grid=(halves, rows // ROWS),
        in_specs=in_specs,
        out_specs=out_specs,
        out_shape=out_shape,
        compiler_params=pltpu.CompilerParams(vmem_limit_bytes=48 * 1024 * 1024),
        cost_estimate=pl.CostEstimate(
            flops=8 * halves * rows * width * keys,
            bytes_accessed=4 * 1024 * 1024,
            transcendentals=halves * rows * keys,
        ),
    )(lens, q, *shards, *extra)


def merge_kernel(sums_ref, stats_ref, message_ref, live_ref, out_ref):
    width, rows = sums_ref.shape
    tokens = out_ref.shape[0]
    tail = message_ref[width : width + 16, :].astype(jnp.float32)
    top_a, total_a = stats_ref[0:1, :], stats_ref[1:2, :]
    top_b = tail[0:1] + tail[1:2] + tail[2:3]
    total_b = tail[3:4] + tail[4:5] + tail[5:6]
    top = jnp.maximum(top_a, top_b)
    a, b = jnp.exp2(top_a - top), jnp.exp2(top_b - top)
    inverse = live_ref[0:1, :] / (total_a * a + total_b * b)
    a, b = a * inverse, b * inverse
    for i in range(rows // 128):
        at = slice(i * 128, (i + 1) * 128)
        block = sums_ref[:, at] * a[:, at] + message_ref[0:width, at].astype(jnp.float32) * b[:, at]
        block = block.T.astype(jnp.bfloat16)
        for part in range(128 // tokens):
            head = i * (128 // tokens) + part
            out_ref[:, head * width : (head + 1) * width] = block[
                part * tokens : (part + 1) * tokens, :
            ]


def merge(sums, stats, message, live, tokens):
    width, rows = sums.shape
    return pl.pallas_call(
        merge_kernel,
        out_shape=jax.ShapeDtypeStruct((tokens, rows // tokens * width), jnp.bfloat16),
        compiler_params=pltpu.CompilerParams(vmem_limit_bytes=48 * 1024 * 1024),
        cost_estimate=pl.CostEstimate(
            flops=4 * width * rows, bytes_accessed=8 * width * rows, transcendentals=2 * rows
        ),
    )(sums, stats, message, live)


def rotate(values, cosine, sine):
    half = values.shape[-1] // 2
    first, second = values[..., :half], values[..., half:]
    return jnp.concatenate(
        [first * cosine - second * sine, second * cosine + first * sine], -1
    ).astype(jnp.bfloat16)


def body(
    queries,
    unrotated_key_rows,
    incoming_value_rows,
    cache_keys,
    stored_value_rows,
    cache_len,
    new_count,
    slot_index,
    out_weight,
):
    ny, nz, nheads = lax.axis_size("y"), lax.axis_size("z"), lax.axis_size("head")
    y, z, core = lax.axis_index("y"), lax.axis_index("z"), lax.axis_index("core")
    convs, slots = slot_index.shape[1], slot_index.shape[2]
    shards = slot_index.shape[0]
    heads, width = queries.shape[1], queries.shape[2]
    here = y * nz + z
    other_core = [(0, 1), (1, 0)]

    small = jnp.concatenate(
        [
            queries.reshape(convs, slots * heads, width),
            unrotated_key_rows.reshape(convs, slots, width),
            incoming_value_rows.reshape(convs, slots, width),
            jnp.broadcast_to(
                cache_len[0].astype(jnp.bfloat16)[:, None, None], (convs, 16 - 2 * slots, width)
            ),
        ],
        1,
    )
    mine = lax.all_to_all(small, ("y", "z"), 0, 0, tiled=True)
    theirs = lax.ppermute(mine, "core", other_core)

    def shard_of(conversation):
        return jnp.concatenate(
            [
                lax.dynamic_index_in_dim(cache_keys[0, :, 0], conversation, 0, keepdims=False),
                lax.dynamic_index_in_dim(
                    stored_value_rows[0, :, 0], conversation, 0, keepdims=False
                ),
            ],
            0,
        )

    def chip_at(dy, dz):
        return (y + dy) % ny * nz + (z + dz) % nz

    def leg(dy, dz):
        route = [
            (a * nz + b, (a + dy) % ny * nz + (b + dz) % nz) for a in range(ny) for b in range(nz)
        ]
        return lax.ppermute(shard_of(chip_at(dy, dz)), ("y", "z"), route)

    arrived = [[leg(dy, dz) for dy, dz in group] for group in LEGS]

    weight_core = lax.ppermute(out_weight, "core", other_core)
    weight_y = lax.ppermute(out_weight, "y", [(0, 1), (1, 0)])
    weight_both = lax.ppermute(weight_y, "core", other_core)
    near = [
        jnp.where(core == 0, out_weight, weight_core),
        jnp.where(core == 0, weight_core, out_weight),
    ]
    far = [
        jnp.where(core == 0, weight_y, weight_both),
        jnp.where(core == 0, weight_both, weight_y),
    ]
    weights = jnp.stack(
        [jnp.where(y == 0, a, b) for a, b in zip(near, far)]
        + [jnp.where(y == 0, b, a) for a, b in zip(near, far)]
    )

    both = jnp.where(core == 0, jnp.stack([mine, theirs], 1), jnp.stack([theirs, mine], 1))
    both = both.reshape(shards, small.shape[1], width)
    lens = both[:, slots * heads + 2 * slots, 0].astype(jnp.float32)
    base = jnp.sum(lens)
    index = lax.dynamic_index_in_dim(slot_index, here, 1, keepdims=False)
    index = index.reshape(shards, 2, slots // 2).transpose(1, 0, 2)
    live = index < new_count[here]
    inverse = 1.0 / 500000.0 ** (jnp.arange(0, width, 2, dtype=jnp.float32) / width)
    angles = (base + index.astype(jnp.float32))[..., None] * inverse
    cosine, sine = jnp.cos(angles), jnp.sin(angles)
    q = both[:, : slots * heads].reshape(shards, 2, slots // 2, heads, width)
    q = q.transpose(1, 3, 0, 2, 4).astype(jnp.float32)
    q = rotate(q, cosine[:, None], sine[:, None])
    tokens = shards * slots // 2
    q = q.reshape(2, heads * tokens, width)

    def new_rows(start):
        rows = both[:, start : start + slots].reshape(shards, 2, slots // 2, width)
        return rows.transpose(1, 0, 2, 3)

    new_k = rotate(new_rows(slots * heads).astype(jnp.float32), cosine, sine)
    new_k = new_k.reshape(2 * tokens, width)
    new_v = new_rows(slots * heads + slots).reshape(2 * tokens, width)
    kept = live & (jnp.arange(shards)[None, :, None] % 2 == core)
    key_index = jnp.where(kept, index.astype(jnp.float32), CLOSED).reshape(2 * tokens, 1)
    key_index = jnp.broadcast_to(key_index, (2 * tokens, 128))
    row_index = jnp.broadcast_to(
        index.astype(jnp.float32).reshape(2, 1, 1, tokens), (2, 8, heads, tokens)
    ).reshape(2, 8, heads * tokens)

    own_lens = mine[:, slots * heads + 2 * slots, 0].astype(jnp.int32)

    def lens_of(group):
        return jnp.stack([own_lens[chip_at(-dy, -dz)] for dy, dz in group])

    state = attend(
        lens_of([(0, 0)]), q, [shard_of(here)], None, (new_k, new_v, key_index, row_index), False
    )
    for group, blocks in zip(LEGS, arrived):
        last = group is LEGS[-1]
        state = attend(lens_of(group), q, blocks, state, None, last)
    sums, stats, message = state

    message = lax.ppermute(
        lax.dynamic_index_in_dim(message, 1 - core, 0, keepdims=False), "core", other_core
    )
    own_half = lambda a: lax.dynamic_index_in_dim(a, core, 0, keepdims=False)
    live_row = jnp.broadcast_to(
        own_half(live).astype(jnp.float32).reshape(1, 1, tokens), (8, heads, tokens)
    ).reshape(8, heads * tokens)
    attended = merge(own_half(sums), own_half(stats), message, live_row, tokens)

    attended = attended.reshape(nheads, tokens // nheads, heads * width)
    up = [(i, (i + 1) % nz) for i in range(nz)]
    down = [(i, (i - 1) % nz) for i in range(nz)]
    held = {0: attended}
    for step in range(1, nz // 2):
        held[-step % nz] = lax.ppermute(held[(1 - step) % nz], "z", up)
        held[step] = lax.ppermute(held[step - 1], "z", down)
    middle = nz // 2
    cut = nheads // 2
    if cut == 0:
        held[middle] = lax.ppermute(held[middle - 1], "z", down)
    else:
        held[middle] = jnp.concatenate(
            [
                lax.ppermute(held[middle + 1][:cut], "z", up),
                lax.ppermute(held[middle - 1][cut:], "z", down),
            ],
            0,
        )

    def project(which):
        rows = jnp.stack([held[k] for k in which], 1)
        rows = rows.reshape(-1, heads * width)
        parts = jnp.einsum("rk,wkn->wrn", rows, weights, preferred_element_type=jnp.float32)
        parts = parts.astype(jnp.bfloat16).reshape(4 * nheads, -1, out_weight.shape[1])
        got = lax.all_to_all(parts, ("y", "core", "head"), 0, 0, tiled=True)
        got = got.reshape(ny, 2, nheads, len(which), tokens // nheads, -1)
        return jnp.sum(got.astype(jnp.float32), 2).astype(jnp.bfloat16)

    early = (0, 1, 2, nz - 2, nz - 1)
    late = tuple(range(3, nz - 2))
    first, second = project(early), project(late)
    order = early + late
    done = jnp.concatenate([first, second], 2)
    done = jnp.stack([done[:, :, order.index(k)] for k in range(nz)], 0)
    done = lax.dynamic_slice_in_dim(jnp.concatenate([done, done], 0), (nz - z) % nz, nz, 0)
    done = done.reshape(nz, ny, 2, shards // nheads, slots // 2, -1)
    done = done.transpose(3, 1, 0, 2, 4, 5)
    return done.reshape(shards // nheads * convs * slots, -1)


def solution(mesh):
    blk, head = mesh.shape["blk"], mesh.shape["head"]
    fine = Mesh(mesh.devices.reshape(2, blk // 4, 2, head), ("y", "z", "core", "head"))
    blk = ("y", "z", "core")
    return jax.shard_map(
        body,
        mesh=fine,
        in_specs=(
            P(blk, "head", None),
            P(blk, "head", None),
            P(blk, "head", None),
            P(blk, None, "head", None, None),
            P(blk, None, "head", None, None),
            P(blk, None),
            P(),
            P(),
            P("head", blk),
        ),
        out_specs=P("head", blk),
        check_vma=False,
    )
```

```python
import functools

import jax
import jax.numpy as jnp
from jax import lax
from jax.experimental import pallas as pl
from jax.experimental.pallas import tpu as pltpu
from jax.sharding import Mesh, PartitionSpec as P

LOG2_E = 1.4426950408889634
ROWS = 256
SHARDS_AT_ONCE = 4
CLOSED = 1.0e9
SHUT = -1.0e30


def attend_kernel(
    as_message, lens_ref, q_ref, kv_ref, new_k_ref, new_v_ref, key_index_ref, row_index_ref, *refs
):
    keys_ref, values_ref = refs[-2:]
    outs = refs[:-2]
    shards, slots, width = kv_ref.shape[0], kv_ref.shape[1] // 2, kv_ref.shape[2]
    scale = LOG2_E / width**0.5
    first_lane = lax.broadcasted_iota(jnp.int32, (slots, width), 1) == 0
    slot = lax.broadcasted_iota(jnp.int32, (slots, width), 0)
    for i in range(shards):
        keys_ref[i, :, 0:width] = kv_ref[i, 0:slots, :]
        shut = first_lane & (slot >= lens_ref[i])
        keys_ref[i, :, width : 2 * width] = jnp.where(shut, SHUT, 0.0).astype(jnp.bfloat16)
        values_ref[i, :, 0:width] = kv_ref[i, slots : 2 * slots, :]
        values_ref[i, :, width : 2 * width] = jnp.ones((slots, width), jnp.bfloat16)
    lane = lax.broadcasted_iota(jnp.int32, (ROWS, width), 1)
    unit = jnp.where(lane == 0, 1.0, 0.0).astype(jnp.bfloat16)
    ones = jnp.ones((new_v_ref.shape[0], width), jnp.bfloat16)
    seen = key_index_ref[0:1, :] <= row_index_ref[...]
    new_v = jnp.concatenate([new_v_ref[...], ones], 1)

    def score(a, b):
        return lax.dot_general(a, b, (((1,), (1,)), ((), ())), preferred_element_type=jnp.float32)

    def rows_step(block, carry):
        at = pl.ds(pl.multiple_of(block * ROWS, ROWS), ROWS)
        q = q_ref[at, :]
        wide = jnp.concatenate([q, unit], 1)
        new_s = jnp.where(seen, score(q, new_k_ref[...]), SHUT)
        top = jnp.max(new_s, axis=1, keepdims=True)
        sums = None
        for start in range(0, shards, SHARDS_AT_ONCE):
            some = slice(start, start + SHARDS_AT_ONCE)
            s = score(wide, keys_ref[some].reshape(SHARDS_AT_ONCE * slots, 2 * width))
            raised = jnp.maximum(top, jnp.max(s, axis=1, keepdims=True))
            low = raised * scale
            if sums is None:
                w = jnp.exp2(new_s * scale - low).astype(jnp.bfloat16)
                sums = jnp.dot(w, new_v, preferred_element_type=jnp.float32)
            else:
                sums = sums * jnp.exp2(top * scale - low)
            w = jnp.exp2(s * scale - low).astype(jnp.bfloat16)
            v = values_ref[some].reshape(SHARDS_AT_ONCE * slots, 2 * width)
            sums = sums + jnp.dot(w, v, preferred_element_type=jnp.float32)
            top = raised
        numerator, total = sums[:, 0:width], sums[:, width : 2 * width]
        if as_message:
            outs[0][at, 0:width] = numerator.astype(jnp.bfloat16)
            tail = jnp.zeros((ROWS, width), jnp.float32)
            for i, value in enumerate((jnp.broadcast_to(top, (ROWS, width)), total)):
                for j in range(3):
                    part = value.astype(jnp.bfloat16).astype(jnp.float32)
                    tail = jnp.where(lane == 3 * i + j, part, tail)
                    value = value - part
            outs[0][at, width : 2 * width] = tail.astype(jnp.bfloat16)
        else:
            outs[0][at, :] = numerator
            outs[1][at, :] = jnp.where(lane == 0, top, total)
        return carry

    lax.fori_loop(0, q_ref.shape[0] // ROWS, rows_step, 0)


def attend(as_message, lens, q, kv, new_k, new_v, key_index, row_index):
    rows, width = q.shape
    shards, slots = kv.shape[0], kv.shape[1] // 2
    if as_message:
        out_shape = [jax.ShapeDtypeStruct((rows, 2 * width), jnp.bfloat16)]
    else:
        out_shape = [jax.ShapeDtypeStruct((rows, width), jnp.float32)] * 2
    vmem = pl.BlockSpec(memory_space=pltpu.VMEM)
    wide = pltpu.VMEM((shards, slots, 2 * width), jnp.bfloat16)
    return pl.pallas_call(
        functools.partial(attend_kernel, as_message),
        in_specs=[pl.BlockSpec(memory_space=pltpu.SMEM)] + [vmem] * 6,
        out_specs=[vmem] * len(out_shape),
        out_shape=out_shape,
        scratch_shapes=[wide, wide],
        compiler_params=pltpu.CompilerParams(vmem_limit_bytes=40 * 1024 * 1024),
        cost_estimate=pl.CostEstimate(
            flops=8 * rows * width * shards * slots,
            bytes_accessed=4 * 1024 * 1024,
            transcendentals=rows * shards * slots,
        ),
    )(lens, q, kv, new_k, new_v, key_index, row_index)


def merge_kernel(sums_ref, stats_ref, message_ref, live_ref, out_ref):
    rows, width = sums_ref.shape
    tokens = out_ref.shape[0]
    scale = LOG2_E / width**0.5
    for head in range(rows // tokens):
        at = slice(head * tokens, (head + 1) * tokens)
        tail = message_ref[at, width : 2 * width].astype(jnp.float32)
        top_a, total_a = stats_ref[at, 0:1], stats_ref[at, 1:2]
        top_b = tail[:, 0:1] + tail[:, 1:2] + tail[:, 2:3]
        total_b = tail[:, 3:4] + tail[:, 4:5] + tail[:, 5:6]
        top = jnp.maximum(top_a, top_b)
        a = jnp.exp2((top_a - top) * scale)
        b = jnp.exp2((top_b - top) * scale)
        inverse = live_ref[:, 0:1] / (total_a * a + total_b * b)
        other = message_ref[at, 0:width].astype(jnp.float32)
        block = sums_ref[at, :] * (a * inverse) + other * (b * inverse)
        out_ref[:, head * width : (head + 1) * width] = block.astype(jnp.bfloat16)


def merge(sums, stats, message, live):
    rows, width = sums.shape
    tokens = live.shape[0]
    return pl.pallas_call(
        merge_kernel,
        out_shape=jax.ShapeDtypeStruct((tokens, rows // tokens * width), jnp.bfloat16),
        compiler_params=pltpu.CompilerParams(vmem_limit_bytes=40 * 1024 * 1024),
        cost_estimate=pl.CostEstimate(
            flops=4 * width * rows, bytes_accessed=14 * width * rows, transcendentals=2 * rows
        ),
    )(sums, stats, message, live)


def rotate(values, cosine, sine):
    half = values.shape[-1] // 2
    first, second = values[..., :half], values[..., half:]
    return jnp.concatenate(
        [first * cosine - second * sine, second * cosine + first * sine], -1
    ).astype(jnp.bfloat16)


def body(
    queries,
    unrotated_key_rows,
    incoming_value_rows,
    cache_keys,
    stored_value_rows,
    cache_len,
    new_count,
    slot_index,
    out_weight,
):
    ny, nz, nheads = lax.axis_size("y"), lax.axis_size("z"), lax.axis_size("head")
    y, z, core = lax.axis_index("y"), lax.axis_index("z"), lax.axis_index("core")
    convs, slots = slot_index.shape[1], slot_index.shape[2]
    shards = slot_index.shape[0]
    heads, width = queries.shape[1], queries.shape[2]
    here = y * nz + z
    other_core = [(0, 1), (1, 0)]

    kv = jnp.concatenate([cache_keys[0, :, 0], stored_value_rows[0, :, 0]], 1)
    kv = lax.all_to_all(kv, ("y", "z"), 0, 0, tiled=True)

    small = jnp.concatenate(
        [
            queries.reshape(convs, slots * heads, width),
            unrotated_key_rows.reshape(convs, slots, width),
            incoming_value_rows.reshape(convs, slots, width),
            jnp.broadcast_to(
                cache_len[0].astype(jnp.bfloat16)[:, None, None], (convs, 16 - 2 * slots, width)
            ),
        ],
        1,
    )

    def leg(dy, dz):
        target = (y - dy) % ny * nz + (z - dz) % nz
        block = lax.dynamic_index_in_dim(small, target, 0, keepdims=False)
        if (dy, dz) == (0, 0):
            return block
        route = [
            ((a + dy) % ny * nz + (b + dz) % nz, a * nz + b) for a in range(ny) for b in range(nz)
        ]
        return lax.ppermute(block, ("y", "z"), route)

    def unroll(values, axis, by):
        size = values.shape[axis]
        twice = jnp.concatenate([values, values], axis)
        return lax.dynamic_slice_in_dim(twice, (size - by) % size, size, axis)

    mine = jnp.stack([leg(dy, dz) for dy in range(ny) for dz in range(nz)])
    mine = mine.reshape((ny, nz) + small.shape[1:])
    theirs = lax.ppermute(mine, "core", other_core)

    weight, _ = lax.optimization_barrier((out_weight, theirs))
    weight_y = lax.ppermute(weight, "y", [(0, 1), (1, 0)])
    weight_core = lax.ppermute(weight, "core", other_core)
    weight_both = lax.ppermute(weight_y, "core", other_core)
    near = [
        jnp.where(core == 0, out_weight, weight_core),
        jnp.where(core == 0, weight_core, out_weight),
    ]
    far = [
        jnp.where(core == 0, weight_y, weight_both),
        jnp.where(core == 0, weight_both, weight_y),
    ]
    weights = jnp.stack(
        [jnp.where(y == 0, a, b) for a, b in zip(near, far)]
        + [jnp.where(y == 0, b, a) for a, b in zip(near, far)]
    )

    both = jnp.where(core == 0, jnp.stack([mine, theirs], 2), jnp.stack([theirs, mine], 2))
    both = unroll(unroll(both, 1, z), 0, y).reshape(shards, small.shape[1], width)
    lens = both[:, slots * heads + 2 * slots, 0]
    base = jnp.sum(lens.astype(jnp.float32))
    own_lens = lax.dynamic_index_in_dim(lens.reshape(shards // 2, 2), core, 1, keepdims=False)
    index = lax.dynamic_index_in_dim(slot_index, here, 1, keepdims=False)
    index = index.reshape(shards, 2, slots // 2).transpose(1, 0, 2)
    live = index < new_count[here]
    inverse = 1.0 / 500000.0 ** (jnp.arange(0, width, 2, dtype=jnp.float32) / width)
    angles = (base + index.astype(jnp.float32))[..., None] * inverse
    cosine, sine = jnp.cos(angles), jnp.sin(angles)
    q = both[:, : slots * heads].reshape(shards, 2, slots // 2, heads, width)
    q = q.transpose(1, 3, 0, 2, 4).astype(jnp.float32)
    q = rotate(q, cosine[:, None], sine[:, None])
    tokens = shards * slots // 2
    q = q.reshape(2, heads * tokens, width)

    def new_rows(start):
        rows = both[:, start : start + slots].reshape(shards, 2, slots // 2, width)
        return rows.transpose(1, 0, 2, 3)

    new_k = rotate(new_rows(slots * heads).astype(jnp.float32), cosine, sine)
    new_k = new_k.reshape(2 * tokens, width)
    new_v = new_rows(slots * heads + slots).reshape(2 * tokens, width)
    kept = live & (jnp.arange(shards)[None, :, None] % 2 == core)
    key_index = jnp.where(kept, index.astype(jnp.float32), CLOSED).reshape(1, 2 * tokens)
    key_index = jnp.broadcast_to(key_index, (8, 2 * tokens))
    row_index = jnp.broadcast_to(
        index.astype(jnp.float32).reshape(2, 1, tokens, 1), (2, ROWS // tokens, tokens, 128)
    ).reshape(2, ROWS, 128)

    def half(a, which):
        return lax.dynamic_index_in_dim(a, which, 0, keepdims=False)

    def attention(as_message, which):
        return attend(
            as_message,
            own_lens.astype(jnp.int32),
            half(q, which),
            kv,
            new_k,
            new_v,
            key_index,
            half(row_index, which),
        )

    (message,) = attention(True, 1 - core)
    message = lax.ppermute(message, "core", other_core)
    sums, stats = attention(False, core)
    live_rows = half(live, core).astype(jnp.float32).reshape(tokens, 1)
    attended = merge(sums, stats, message, jnp.broadcast_to(live_rows, (tokens, 128)))

    attended = attended.reshape(nheads, tokens // nheads, heads * width)
    up = [(i, (i + 1) % nz) for i in range(nz)]
    down = [(i, (i - 1) % nz) for i in range(nz)]
    held = {0: attended}
    for step in range(1, nz // 2):
        held[-step % nz] = lax.ppermute(held[(1 - step) % nz], "z", up)
        held[step] = lax.ppermute(held[step - 1], "z", down)
    def parts_of(which):
        rows = jnp.stack([held[k] for k in which], 1)
        rows = rows.reshape(-1, heads * width)
        parts = jnp.einsum("rk,wkn->wrn", rows, weights, preferred_element_type=jnp.float32)
        return parts.astype(jnp.bfloat16).reshape(4 * nheads, -1, out_weight.shape[1])

    def over_heads(parts, which):
        got = lax.all_to_all(parts, ("y", "core", "head"), 0, 0, tiled=True)
        got = got.reshape(ny, 2, nheads, len(which), tokens // nheads, -1)
        return jnp.sum(got.astype(jnp.float32), 2).astype(jnp.bfloat16)

    early = (0, 1, 2, nz - 2, nz - 1)
    late = tuple(range(3, nz - 2))
    early_parts = parts_of(early)
    middle = nz // 2
    from_below, from_above, early_parts = lax.optimization_barrier(
        (held[middle + 1], held[middle - 1], early_parts)
    )
    cut = max(nheads // 2, 1)
    held[middle] = jnp.concatenate(
        [
            lax.ppermute(from_below[:cut], "z", up),
            lax.ppermute(from_above[cut:], "z", down),
        ],
        0,
    )
    first = over_heads(early_parts, early)
    second = over_heads(parts_of(late), late)
    order = early + late
    done = jnp.concatenate([first, second], 2)
    done = unroll(jnp.stack([done[:, :, order.index(k)] for k in range(nz)], 0), 0, z)
    done = done.reshape(nz, ny, 2, shards // nheads, slots // 2, -1)
    done = done.transpose(3, 1, 0, 2, 4, 5)
    return done.reshape(shards // nheads * convs * slots, -1)


def solution(mesh):
    blk, head = mesh.shape["blk"], mesh.shape["head"]
    fine = Mesh(mesh.devices.reshape(2, blk // 4, 2, head), ("y", "z", "core", "head"))
    blk = ("y", "z", "core")
    return jax.shard_map(
        body,
        mesh=fine,
        in_specs=(
            P(blk, "head", None),
            P(blk, "head", None),
            P(blk, "head", None),
            P(blk, None, "head", None, None),
            P(blk, None, "head", None, None),
            P(blk, None),
            P(),
            P(),
            P("head", blk),
        ),
        out_specs=P("head", blk),
        check_vma=False,
    )
```

```python
import functools

import jax
import jax.numpy as jnp
from jax import lax
from jax.experimental import pallas as pl
from jax.experimental.pallas import tpu as pltpu
from jax.sharding import Mesh, PartitionSpec as P

LOG2_E = 1.4426950408889634
CLOSED = 1.0e9
SHUT = -1.0e30
STEP = 256
LEGS = (
    ((0, 4), (1, 4), (0, 3), (0, -3)),
    ((1, 3), (1, -3), (0, 2), (0, -2)),
    ((1, 2), (1, -2), (0, 1), (0, -1)),
    ((1, 1), (1, -1), (1, 0)),
)


def deal_kernel(targets, at_ref, keys_ref, values_ref, *refs):
    outs, sems = refs[:-1], refs[-1]
    ny, nz = targets[0]
    copies = []
    for i, (dy, dz) in enumerate(targets[1]):
        conversation = lax.rem(at_ref[0] + dy, ny) * nz + lax.rem(at_ref[1] + (dz + nz) % nz, nz)
        slots = keys_ref.shape[3]
        for j, ref in enumerate((keys_ref, values_ref)):
            copies.append(
                pltpu.make_async_copy(
                    ref.at[0, conversation, 0],
                    outs[i].at[pl.ds(j * slots, slots)],
                    sems.at[i, j],
                )
            )
    for copy in copies:
        copy.start()
    for copy in copies:
        copy.wait()


def deal(at, keys, values, grid, targets):
    slots, width = keys.shape[3], keys.shape[4]
    anywhere = pl.BlockSpec(memory_space=pl.ANY)
    return pl.pallas_call(
        functools.partial(deal_kernel, (grid, targets)),
        in_specs=[pl.BlockSpec(memory_space=pltpu.SMEM), anywhere, anywhere],
        out_specs=[anywhere] * len(targets),
        out_shape=[jax.ShapeDtypeStruct((2 * slots, width), jnp.bfloat16)] * len(targets),
        scratch_shapes=[pltpu.SemaphoreType.DMA((len(targets), 2))],
    )(at, keys, values)


def attend_kernel(first_len, shards, first, as_message, plan_ref, q_ref, *refs):
    refs = list(refs)
    keys_ref, values_ref = refs[-2:]
    kv_refs = [refs.pop(0) for _ in range(shards)]
    if first:
        new_k_ref, new_v_ref, key_index_ref, row_index_ref = [refs.pop(0) for _ in range(4)]
    else:
        sums_ref = refs.pop(0)
    out_ref = refs.pop(0)
    rows, width = q_ref.shape[1], q_ref.shape[2]
    slots = kv_refs[0].shape[0] // 2
    scale = LOG2_E / width**0.5

    @pl.when(pl.program_id(0) == 0)
    def _():
        first_lane = lax.broadcasted_iota(jnp.int32, (slots, width), 1) == 0
        slot = lax.broadcasted_iota(jnp.int32, (slots, width), 0)
        for i, ref in enumerate(kv_refs):
            at = slice(i * slots, (i + 1) * slots)
            keys_ref[at, 0:width] = ref[0:slots, :]
            shut = first_lane & (slot >= plan_ref[first_len + i])
            keys_ref[at, width : 2 * width] = jnp.where(shut, SHUT, 0.0).astype(jnp.bfloat16)
            values_ref[at, 0:width] = ref[slots : 2 * slots, :]
            values_ref[at, width : 2 * width] = jnp.ones((slots, width), jnp.bfloat16)

    lane = lax.broadcasted_iota(jnp.int32, (STEP, width), 1)
    unit = jnp.where(lane == 0, 1.0, 0.0).astype(jnp.bfloat16)
    if first:
        seen = key_index_ref[0:1, :] <= row_index_ref[0]
        ones = jnp.ones((new_v_ref.shape[0], width), jnp.bfloat16)

    def score(a, b):
        return lax.dot_general(a, b, (((1,), (1,)), ((), ())), preferred_element_type=jnp.float32)

    def scores(step):
        q = q_ref[0, step * STEP : (step + 1) * STEP, :]
        wide = jnp.concatenate([q, unit], 1)
        found = [score(wide, keys_ref[i * slots : (i + 1) * slots, :]) for i in range(shards)]
        if first:
            found.append(jnp.where(seen, score(q, new_k_ref[...]), SHUT))
        return found

    def highest(found, step):
        top = jnp.max(functools.reduce(jnp.maximum, found[:shards]), axis=1, keepdims=True)
        if first:
            return jnp.maximum(top, jnp.max(found[shards], axis=1, keepdims=True))
        before = sums_ref[0, step * STEP : (step + 1) * STEP, 2 * width - 1 : 2 * width]
        return jnp.maximum(top, before)

    steps = rows // STEP
    after = scores(0)
    after_top = highest(after, 0)
    for step in range(steps):
        at = slice(step * STEP, (step + 1) * STEP)
        found, top = after, after_top
        if step + 1 < steps:
            after = scores(step + 1)
        low = top * scale
        if first:
            sums = jnp.zeros((STEP, 2 * width), jnp.float32)
        else:
            sums = sums_ref[0, at, :]
            sums = sums * jnp.exp2(sums[:, 2 * width - 1 : 2 * width] * scale - low)
        for i, s in enumerate(found):
            w = jnp.exp2(s * scale - low).astype(jnp.bfloat16)
            if i < shards:
                v = values_ref[i * slots : (i + 1) * slots, :]
            else:
                v = jnp.concatenate([new_v_ref[...], ones], 1)
            sums = sums + jnp.dot(w, v, preferred_element_type=jnp.float32)
        if step + 1 < steps:
            after_top = highest(after, step + 1)
        if as_message:
            out_ref[at, 0:width] = sums[:, 0:width].astype(jnp.bfloat16)
            tail = jnp.zeros((STEP, width), jnp.float32)
            total = sums[:, width : width + 1]
            for i, value in enumerate((total, top)):
                for j in range(3):
                    part = value.astype(jnp.bfloat16).astype(jnp.float32)
                    tail = jnp.where(lane == 3 * i + j, part, tail)
                    value = value - part
            out_ref[at, width : 2 * width] = tail.astype(jnp.bfloat16)
        else:
            out_ref[0, at, 0:width] = sums[:, 0:width]
            out_ref[0, at, width : 2 * width] = jnp.where(
                lane < width // 2, sums[:, width : 2 * width], top
            )


def attend(first_len, plan, q, kv, sums, new, halves, as_message=False):
    both, rows, width = q.shape
    slots = kv[0].shape[0] // 2
    part = lambda *tail: pl.BlockSpec((1,) + tail, lambda i, s: (lax.rem(s[0] + i, both), 0, 0))
    whole = lambda a: pl.BlockSpec(a.shape, lambda i, s: (0, 0))
    in_specs = [part(rows, width)] + [whole(a) for a in kv]
    if sums is None:
        in_specs += [whole(a) for a in new[:3]] + [part(*new[3].shape[1:])]
        extra = tuple(new)
    else:
        in_specs.append(part(rows, 2 * width))
        extra = (sums,)
    if as_message:
        out_shape = jax.ShapeDtypeStruct((rows, 2 * width), jnp.bfloat16)
        out_spec = pl.BlockSpec((rows, 2 * width), lambda i, s: (0, 0))
    elif halves == 1:
        out_shape = jax.ShapeDtypeStruct((1, rows, 2 * width), jnp.float32)
        out_spec = pl.BlockSpec((1, rows, 2 * width), lambda i, s: (0, 0, 0))
    else:
        out_shape = jax.ShapeDtypeStruct((both, rows, 2 * width), jnp.float32)
        out_spec = part(rows, 2 * width)
    wide = pltpu.VMEM((len(kv) * slots, 2 * width), jnp.bfloat16)
    keys = len(kv) * slots
    return pl.pallas_call(
        functools.partial(attend_kernel, first_len, len(kv), sums is None, as_message),
        grid_spec=pltpu.PrefetchScalarGridSpec(
            num_scalar_prefetch=1,
            grid=(halves,),
            in_specs=in_specs,
            out_specs=out_spec,
            scratch_shapes=[wide, wide],
        ),
        out_shape=out_shape,
        compiler_params=pltpu.CompilerParams(vmem_limit_bytes=40 * 1024 * 1024),
        cost_estimate=pl.CostEstimate(
            flops=16 * halves * rows * width * keys,
            bytes_accessed=halves * rows * width * 16,
            transcendentals=halves * rows * keys,
        ),
    )(plan, q, *kv, *extra)


def merge_kernel(sums_ref, message_ref, live_ref, out_ref):
    rows, width = sums_ref.shape[1], sums_ref.shape[2] // 2
    tokens = out_ref.shape[0]
    scale = LOG2_E / width**0.5
    for head in range(rows // tokens):
        at = slice(head * tokens, (head + 1) * tokens)
        tail = message_ref[at, width : 2 * width].astype(jnp.float32)
        total_a, top_a = sums_ref[0, at, width : width + 1], sums_ref[0, at, 2 * width - 1 :]
        total_b = tail[:, 0:1] + tail[:, 1:2] + tail[:, 2:3]
        top_b = tail[:, 3:4] + tail[:, 4:5] + tail[:, 5:6]
        top = jnp.maximum(top_a, top_b)
        a = jnp.exp2((top_a - top) * scale)
        b = jnp.exp2((top_b - top) * scale)
        inverse = live_ref[:, 0:1] / (total_a * a + total_b * b)
        other = message_ref[at, 0:width].astype(jnp.float32)
        block = sums_ref[0, at, 0:width] * (a * inverse) + other * (b * inverse)
        out_ref[:, head * width : (head + 1) * width] = block.astype(jnp.bfloat16)


def merge(sums, message, live):
    rows, width = sums.shape[1], sums.shape[2] // 2
    tokens = live.shape[0]
    return pl.pallas_call(
        merge_kernel,
        out_shape=jax.ShapeDtypeStruct((tokens, rows // tokens * width), jnp.bfloat16),
        compiler_params=pltpu.CompilerParams(vmem_limit_bytes=40 * 1024 * 1024),
        cost_estimate=pl.CostEstimate(
            flops=4 * width * rows, bytes_accessed=14 * width * rows, transcendentals=2 * rows
        ),
    )(sums, message, live)


def rotate(values, cosine, sine):
    half = values.shape[-1] // 2
    first, second = values[..., :half], values[..., half:]
    return jnp.concatenate(
        [first * cosine - second * sine, second * cosine + first * sine], -1
    ).astype(jnp.bfloat16)


def body(
    queries,
    unrotated_key_rows,
    incoming_value_rows,
    cache_keys,
    stored_value_rows,
    cache_len,
    new_count,
    slot_index,
    out_weight,
):
    ny, nz, nheads = lax.axis_size("y"), lax.axis_size("z"), lax.axis_size("head")
    y, z, core = lax.axis_index("y"), lax.axis_index("z"), lax.axis_index("core")
    convs, slots = slot_index.shape[1], slot_index.shape[2]
    shards = slot_index.shape[0]
    heads, width = queries.shape[1], queries.shape[2]
    here = y * nz + z
    other_core = [(0, 1), (1, 0)]

    def unroll(values, axis, by):
        size = values.shape[axis]
        twice = jnp.concatenate([values, values], axis)
        return lax.dynamic_slice_in_dim(twice, (size - by) % size, size, axis)

    small = jnp.concatenate(
        [
            queries.reshape(convs, slots * heads, width),
            unrotated_key_rows.reshape(convs, slots, width),
            incoming_value_rows.reshape(convs, slots, width),
            jnp.broadcast_to(
                cache_len[0].astype(jnp.bfloat16)[:, None, None], (convs, 16 - 2 * slots, width)
            ),
        ],
        1,
    )
    mine = lax.all_to_all(small, ("y", "z"), 0, 0, tiled=True)
    theirs = lax.ppermute(mine, "core", other_core)

    targets = ((0, 0),) + tuple(leg for group in LEGS for leg in group)
    at = jnp.stack([y, z]).astype(jnp.int32)
    dealt = dict(zip(targets, deal(at, cache_keys, stored_value_rows, (ny, nz), targets)))

    def sent(dy, dz):
        route = [
            (a * nz + b, (a + dy) % ny * nz + (b + dz) % nz) for a in range(ny) for b in range(nz)
        ]
        return lax.ppermute(dealt[dy, dz], ("y", "z"), route)

    arrived = [[sent(*leg) for leg in group] for group in LEGS]

    weights = lax.all_gather(out_weight, ("y", "core"), axis=0)

    both = jnp.where(core == 0, jnp.stack([mine, theirs], 1), jnp.stack([theirs, mine], 1))
    both = both.reshape(shards, small.shape[1], width)
    base = jnp.sum(both[:, slots * heads + 2 * slots, 0].astype(jnp.float32))
    own_lens = mine[:, slots * heads + 2 * slots, 0].astype(jnp.int32)
    senders = [(y - dy) % ny * nz + (z - dz) % nz for dy, dz in targets]
    own_lens = jnp.sum(
        jnp.where(jnp.stack(senders)[:, None] == jnp.arange(convs), own_lens[None, :], 0), 1
    )
    index = lax.dynamic_index_in_dim(slot_index, here, 1, keepdims=False)
    index = index.reshape(shards, 2, slots // 2).transpose(1, 0, 2)
    live = index < new_count[here]
    inverse = 1.0 / 500000.0 ** (jnp.arange(0, width, 2, dtype=jnp.float32) / width)
    angles = (base + index.astype(jnp.float32))[..., None] * inverse
    cosine, sine = jnp.cos(angles), jnp.sin(angles)
    q = both[:, : slots * heads].reshape(shards, 2, slots // 2, heads, width)
    q = q.transpose(1, 3, 0, 2, 4).astype(jnp.float32)
    q = rotate(q, cosine[:, None], sine[:, None])
    tokens = shards * slots // 2
    q = q.reshape(2, heads * tokens, width)

    def new_rows(start):
        rows = both[:, start : start + slots].reshape(shards, 2, slots // 2, width)
        return rows.transpose(1, 0, 2, 3)

    new_k = rotate(new_rows(slots * heads).astype(jnp.float32), cosine, sine)
    new_k = new_k.reshape(2 * tokens, width)
    new_v = new_rows(slots * heads + slots).reshape(2 * tokens, width)
    kept = live & (jnp.arange(shards)[None, :, None] % 2 == core)
    key_index = jnp.where(kept, index.astype(jnp.float32), CLOSED).reshape(1, 2 * tokens)
    key_index = jnp.broadcast_to(key_index, (8, 2 * tokens))
    row_index = jnp.broadcast_to(
        index.astype(jnp.float32).reshape(2, 1, tokens, 1), (2, STEP // tokens, tokens, 128)
    ).reshape(2, STEP, 128)

    def plan(which):
        return jnp.concatenate([jnp.full((1,), which, jnp.int32), own_lens])

    start = plan(0)
    sums = attend(1, start, q, [dealt[0, 0]], None, (new_k, new_v, key_index, row_index), 2)
    at_len = 2
    for blocks in arrived[:-1]:
        sums = attend(at_len, start, q, blocks, sums, None, 2)
        at_len += len(blocks)
    message = attend(at_len, plan(1 - core), q, arrived[-1], sums, None, 1, True)
    message = lax.ppermute(message, "core", other_core)
    sums = attend(at_len, plan(core), q, arrived[-1], sums, None, 1)
    live_rows = lax.dynamic_index_in_dim(live, core, 0, keepdims=False)
    live_rows = live_rows.astype(jnp.float32).reshape(tokens, 1)
    attended = merge(sums, message, jnp.broadcast_to(live_rows, (tokens, 128)))

    attended = attended.reshape(nheads, tokens // nheads, heads * width)
    up = [(i, (i + 1) % nz) for i in range(nz)]
    down = [(i, (i - 1) % nz) for i in range(nz)]
    held = {0: attended}
    for step in range(1, nz // 2):
        held[-step % nz] = lax.ppermute(held[(1 - step) % nz], "z", up)
        held[step] = lax.ppermute(held[step - 1], "z", down)
    def parts_of(which):
        rows = jnp.stack([held[k] for k in which], 1)
        rows = rows.reshape(-1, heads * width)
        parts = jnp.einsum("rk,wkn->wrn", rows, weights, preferred_element_type=jnp.float32)
        return parts.astype(jnp.bfloat16).reshape(4 * nheads, -1, out_weight.shape[1])

    early = (0, 1, 2, nz - 2, nz - 1)
    late = tuple(range(3, nz - 2))
    early_parts = parts_of(early)
    middle = nz // 2
    from_below, from_above, early_parts = lax.optimization_barrier(
        (held[middle + 1], held[middle - 1], early_parts)
    )
    cut = max(nheads // 2, 1)
    held[middle] = jnp.concatenate(
        [
            lax.ppermute(from_below[:cut], "z", up),
            lax.ppermute(from_above[cut:], "z", down),
        ],
        0,
    )
    parts = jnp.concatenate([early_parts, parts_of(late)], 1)
    got = lax.all_to_all(parts, ("y", "core", "head"), 0, 0, tiled=True)
    got = got.reshape(ny, 2, nheads, nz, tokens // nheads, -1)
    done = jnp.sum(got.astype(jnp.float32), 2).astype(jnp.bfloat16)
    order = early + late
    done = unroll(jnp.stack([done[:, :, order.index(k)] for k in range(nz)], 0), 0, z)
    done = done.reshape(nz, ny, 2, shards // nheads, slots // 2, -1)
    done = done.transpose(3, 1, 0, 2, 4, 5)
    return done.reshape(shards // nheads * convs * slots, -1)


def solution(mesh):
    blk, head = mesh.shape["blk"], mesh.shape["head"]
    fine = Mesh(mesh.devices.reshape(2, blk // 4, 2, head), ("y", "z", "core", "head"))
    blk = ("y", "z", "core")
    return jax.shard_map(
        body,
        mesh=fine,
        in_specs=(
            P(blk, "head", None),
            P(blk, "head", None),
            P(blk, "head", None),
            P(blk, None, "head", None, None),
            P(blk, None, "head", None, None),
            P(blk, None),
            P(),
            P(),
            P("head", blk),
        ),
        out_specs=P("head", blk),
        check_vma=False,
    )
```

```python
import functools

import jax
import jax.numpy as jnp
from jax import lax
from jax.experimental import pallas as pl
from jax.experimental.pallas import tpu as pltpu
from jax.sharding import Mesh, PartitionSpec as P

LOG2_E = 1.4426950408889634
CLOSED = 1.0e9
SHUT = -1.0e30
STEP = 256
LEGS = (
    ((0, 4), (1, 4), (0, 3), (0, -3)),
    ((1, 3), (1, -3), (0, 2), (0, -2)),
    ((1, 2), (1, -2), (0, 1), (0, -1)),
    ((1, 1), (1, -1), (1, 0)),
)


def deal_kernel(targets, at_ref, keys_ref, values_ref, *refs):
    outs, (stage, in_sems, out_sems) = refs[:-3], refs[-3:]
    ny, nz = targets[0]
    slots = keys_ref.shape[3]
    copies = []
    for i, (dy, dz) in enumerate(targets[1]):
        conversation = lax.rem(at_ref[0] + dy, ny) * nz + lax.rem(at_ref[1] + (dz + nz) % nz, nz)
        for j, ref in enumerate((keys_ref, values_ref)):
            copy = pltpu.make_async_copy(
                ref.at[0, conversation, 0], stage.at[i, pl.ds(j * slots, slots)], in_sems.at[i, j]
            )
            copy.start()
            copies.append(copy)
    leaving = []
    for i in range(len(outs)):
        copies[2 * i].wait()
        copies[2 * i + 1].wait()
        copy = pltpu.make_async_copy(stage.at[i], outs[i], out_sems.at[i])
        copy.start()
        leaving.append(copy)
    for copy in leaving:
        copy.wait()


def deal(at, keys, values, grid, targets):
    slots, width = keys.shape[3], keys.shape[4]
    anywhere = pl.BlockSpec(memory_space=pl.ANY)
    count = len(targets)
    return pl.pallas_call(
        functools.partial(deal_kernel, (grid, targets)),
        in_specs=[pl.BlockSpec(memory_space=pltpu.SMEM), anywhere, anywhere],
        out_specs=[anywhere] * count,
        out_shape=[jax.ShapeDtypeStruct((2 * slots, width), jnp.bfloat16)] * count,
        scratch_shapes=[
            pltpu.VMEM((count, 2 * slots, width), jnp.bfloat16),
            pltpu.SemaphoreType.DMA((count, 2)),
            pltpu.SemaphoreType.DMA((count,)),
        ],
    )(at, keys, values)


def attend_kernel(first_len, shards, first, last, plan_ref, q_ref, *refs):
    refs = list(refs)
    keys_ref, values_ref = refs[-2:]
    kv_refs = [refs.pop(0) for _ in range(shards)]
    if first:
        new_k_ref, new_v_ref, key_index_ref, row_index_ref = [refs.pop(0) for _ in range(4)]
    else:
        sums_ref = refs.pop(0)
    out_ref, tail_ref = refs.pop(0), refs[0]
    rows, width = q_ref.shape[1], q_ref.shape[2]
    slots = kv_refs[0].shape[0] // 2
    scale = LOG2_E / width**0.5

    @pl.when(pl.program_id(0) == 0)
    def _():
        first_lane = lax.broadcasted_iota(jnp.int32, (slots, width), 1) == 0
        slot = lax.broadcasted_iota(jnp.int32, (slots, width), 0)
        for i, ref in enumerate(kv_refs):
            at = slice(i * slots, (i + 1) * slots)
            keys_ref[at, 0:width] = ref[0:slots, :]
            shut = first_lane & (slot >= plan_ref[first_len + i])
            keys_ref[at, width : 2 * width] = jnp.where(shut, SHUT, 0.0).astype(jnp.bfloat16)
            values_ref[at, 0:width] = ref[slots : 2 * slots, :]
            values_ref[at, width : 2 * width] = jnp.ones((slots, width), jnp.bfloat16)

    lane = lax.broadcasted_iota(jnp.int32, (STEP, width), 1)
    unit = jnp.where(lane == 0, 1.0, 0.0).astype(jnp.bfloat16)
    if first:
        seen = key_index_ref[0:1, :] <= row_index_ref[0]
        ones = jnp.ones((new_v_ref.shape[0], width), jnp.bfloat16)

    def score(a, b):
        return lax.dot_general(a, b, (((1,), (1,)), ((), ())), preferred_element_type=jnp.float32)

    def scores(step):
        q = q_ref[0, step * STEP : (step + 1) * STEP, :]
        wide = jnp.concatenate([q, unit], 1)
        found = [score(wide, keys_ref[i * slots : (i + 1) * slots, :]) for i in range(shards)]
        if first:
            found.append(jnp.where(seen, score(q, new_k_ref[...]), SHUT))
        return found

    def highest(found, step):
        top = jnp.max(functools.reduce(jnp.maximum, found[:shards]), axis=1, keepdims=True)
        if first:
            return jnp.maximum(top, jnp.max(found[shards], axis=1, keepdims=True))
        before = sums_ref[0, step * STEP : (step + 1) * STEP, 2 * width - 1 : 2 * width]
        return jnp.maximum(top, before)

    steps = rows // STEP
    after = scores(0)
    after_top = highest(after, 0)
    for step in range(steps):
        at = slice(step * STEP, (step + 1) * STEP)
        found, top = after, after_top
        if step + 1 < steps:
            after = scores(step + 1)
        low = top * scale
        if first:
            sums = jnp.zeros((STEP, 2 * width), jnp.float32)
        else:
            sums = sums_ref[0, at, :]
            sums = sums * jnp.exp2(sums[:, 2 * width - 1 : 2 * width] * scale - low)
        for i, s in enumerate(found):
            w = jnp.exp2(s * scale - low).astype(jnp.bfloat16)
            if i < shards:
                v = values_ref[i * slots : (i + 1) * slots, :]
            else:
                v = jnp.concatenate([new_v_ref[...], ones], 1)
            sums = sums + jnp.dot(w, v, preferred_element_type=jnp.float32)
        if step + 1 < steps:
            after_top = highest(after, step + 1)
        if last:
            tail = jnp.zeros((STEP, width), jnp.float32)
            total = sums[:, width : 2 * width]
            for i, value in enumerate((total, jnp.broadcast_to(top, total.shape))):
                for j in range(3):
                    part = value.astype(jnp.bfloat16).astype(jnp.float32)
                    tail = jnp.where(lane == 3 * i + j, part, tail)
                    value = value - part
            tail = tail.astype(jnp.bfloat16)
            out_ref[at, 0:width] = sums[:, 0:width].astype(out_ref.dtype)
            if out_ref.shape[1] == 2 * width:
                out_ref[at, width : 2 * width] = tail
            else:
                tail_ref[at, :] = tail
        else:
            out_ref[0, at, 0:width] = sums[:, 0:width]
            out_ref[0, at, width : 2 * width] = jnp.where(
                lane < width // 2, sums[:, width : 2 * width], top
            )


def attend(first_len, plan, q, kv, sums, new, halves, last=False, as_message=False):
    both, rows, width = q.shape
    slots = kv[0].shape[0] // 2
    part = lambda *tail: pl.BlockSpec((1,) + tail, lambda i, s: (lax.rem(s[0] + i, both), 0, 0))
    whole = lambda a: pl.BlockSpec(a.shape, lambda i, s: (0, 0))
    in_specs = [part(rows, width)] + [whole(a) for a in kv]
    if sums is None:
        in_specs += [whole(a) for a in new[:3]] + [part(*new[3].shape[1:])]
        extra = tuple(new)
    else:
        in_specs.append(part(rows, 2 * width))
        extra = (sums,)
    if last:
        fixed = lambda a: pl.BlockSpec(a.shape, lambda i, s: (0, 0))
        if as_message:
            out_shape = [jax.ShapeDtypeStruct((rows, 2 * width), jnp.bfloat16)]
        else:
            out_shape = [
                jax.ShapeDtypeStruct((rows, width), jnp.float32),
                jax.ShapeDtypeStruct((rows, width), jnp.bfloat16),
            ]
        out_spec = [fixed(a) for a in out_shape]
    else:
        out_shape = jax.ShapeDtypeStruct((both, rows, 2 * width), jnp.float32)
        out_spec = part(rows, 2 * width)
    wide = pltpu.VMEM((len(kv) * slots, 2 * width), jnp.bfloat16)
    keys = len(kv) * slots
    return pl.pallas_call(
        functools.partial(attend_kernel, first_len, len(kv), sums is None, last),
        grid_spec=pltpu.PrefetchScalarGridSpec(
            num_scalar_prefetch=1,
            grid=(halves,),
            in_specs=in_specs,
            out_specs=out_spec,
            scratch_shapes=[wide, wide],
        ),
        out_shape=out_shape,
        compiler_params=pltpu.CompilerParams(vmem_limit_bytes=40 * 1024 * 1024),
        cost_estimate=pl.CostEstimate(
            flops=16 * halves * rows * width * keys,
            bytes_accessed=halves * rows * width * 16,
            transcendentals=halves * rows * keys,
        ),
    )(plan, q, *kv, *extra)


def merge_kernel(sums_ref, tail_ref, message_ref, live_ref, out_ref):
    rows, width = sums_ref.shape
    tokens = live_ref.shape[0]
    scale = LOG2_E / width**0.5
    lane = lax.broadcasted_iota(jnp.int32, (width, 2 * width), 0)
    column = lax.broadcasted_iota(jnp.int32, (width, 2 * width), 1)
    group = jnp.where(column < width, 0, 3)
    spread = jnp.where((lane >= group) & (lane < group + 3), 1.0, 0.0).astype(jnp.bfloat16)
    stats_a = jnp.dot(tail_ref[...], spread, preferred_element_type=jnp.float32)
    tail_b = message_ref[:, width : 2 * width]
    stats_b = jnp.dot(tail_b, spread, preferred_element_type=jnp.float32)
    top_a, top_b = stats_a[:, width:], stats_b[:, width:]
    top = jnp.maximum(top_a, top_b)
    a = jnp.exp2((top_a - top) * scale)
    b = jnp.exp2((top_b - top) * scale)
    total = stats_a[:, :width] * a + stats_b[:, :width] * b
    mixed = (sums_ref[...] * a + message_ref[:, 0:width].astype(jnp.float32) * b) / total
    for head in range(rows // tokens):
        block = mixed[head * tokens : (head + 1) * tokens, :] * live_ref[...]
        out_ref[:, head * width : (head + 1) * width] = block.astype(jnp.bfloat16)


def merge(sums, tail, message, live):
    rows, width = sums.shape
    tokens = live.shape[0]
    steps = 4 if rows % (4 * tokens) == 0 else 1
    high = lambda a: pl.BlockSpec((rows // steps, a.shape[1]), lambda i: (i, 0))
    wide = rows // tokens * width
    return pl.pallas_call(
        merge_kernel,
        grid=(steps,),
        in_specs=[high(sums), high(tail), high(message), pl.BlockSpec(live.shape, lambda i: (0, 0))],
        out_specs=pl.BlockSpec((tokens, wide // steps), lambda i: (0, i)),
        out_shape=jax.ShapeDtypeStruct((tokens, wide), jnp.bfloat16),
        cost_estimate=pl.CostEstimate(
            flops=4 * width * rows, bytes_accessed=14 * width * rows, transcendentals=2 * rows
        ),
    )(sums, tail, message, live)


def rotate(values, cosine, sine):
    half = values.shape[-1] // 2
    first, second = values[..., :half], values[..., half:]
    return jnp.concatenate(
        [first * cosine - second * sine, second * cosine + first * sine], -1
    ).astype(jnp.bfloat16)


def body(
    queries,
    unrotated_key_rows,
    incoming_value_rows,
    cache_keys,
    stored_value_rows,
    cache_len,
    new_count,
    slot_index,
    out_weight,
):
    ny, nz, nheads = lax.axis_size("y"), lax.axis_size("z"), lax.axis_size("head")
    y, z, core = lax.axis_index("y"), lax.axis_index("z"), lax.axis_index("core")
    convs, slots = slot_index.shape[1], slot_index.shape[2]
    shards = slot_index.shape[0]
    heads, width = queries.shape[1], queries.shape[2]
    here = y * nz + z
    other_core = [(0, 1), (1, 0)]

    def unroll(values, axis, by):
        size = values.shape[axis]
        twice = jnp.concatenate([values, values], axis)
        return lax.dynamic_slice_in_dim(twice, (size - by) % size, size, axis)

    small = jnp.concatenate(
        [
            queries.reshape(convs, slots * heads, width),
            unrotated_key_rows.reshape(convs, slots, width),
            incoming_value_rows.reshape(convs, slots, width),
            jnp.broadcast_to(
                cache_len[0].astype(jnp.bfloat16)[:, None, None], (convs, 16 - 2 * slots, width)
            ),
        ],
        1,
    )
    mine = lax.all_to_all(small, ("y", "z"), 0, 0, tiled=True)
    theirs = lax.ppermute(mine, "core", other_core)

    targets = ((0, 0),) + tuple(leg for group in LEGS for leg in group)
    at = jnp.stack([y, z]).astype(jnp.int32)
    dealt = dict(zip(targets, deal(at, cache_keys, stored_value_rows, (ny, nz), targets)))

    def sent(dy, dz):
        route = [
            (a * nz + b, (a + dy) % ny * nz + (b + dz) % nz) for a in range(ny) for b in range(nz)
        ]
        return lax.ppermute(dealt[dy, dz], ("y", "z"), route)

    arrived = [[sent(*leg) for leg in group] for group in LEGS]

    weight_y = lax.ppermute(out_weight, "y", [(0, 1), (1, 0)])
    weight_core = lax.ppermute(out_weight, "core", other_core)
    weight_y, _ = lax.optimization_barrier((weight_y, arrived[2][0]))
    weight_both = lax.ppermute(weight_y, "core", other_core)
    near = [
        jnp.where(core == 0, out_weight, weight_core),
        jnp.where(core == 0, weight_core, out_weight),
    ]
    far = [
        jnp.where(core == 0, weight_y, weight_both),
        jnp.where(core == 0, weight_both, weight_y),
    ]
    weights = jnp.stack(
        [jnp.where(y == 0, a, b) for a, b in zip(near, far)]
        + [jnp.where(y == 0, b, a) for a, b in zip(near, far)]
    )

    both = jnp.where(core == 0, jnp.stack([mine, theirs], 1), jnp.stack([theirs, mine], 1))
    both = both.reshape(shards, small.shape[1], width)
    base = jnp.sum(both[:, slots * heads + 2 * slots, 0].astype(jnp.float32))
    own_lens = mine[:, slots * heads + 2 * slots, 0].astype(jnp.int32)
    senders = [(y - dy) % ny * nz + (z - dz) % nz for dy, dz in targets]
    own_lens = jnp.sum(
        jnp.where(jnp.stack(senders)[:, None] == jnp.arange(convs), own_lens[None, :], 0), 1
    )
    index = lax.dynamic_index_in_dim(slot_index, here, 1, keepdims=False)
    index = index.reshape(shards, 2, slots // 2).transpose(1, 0, 2)
    live = index < new_count[here]
    inverse = 1.0 / 500000.0 ** (jnp.arange(0, width, 2, dtype=jnp.float32) / width)
    angles = (base + index.astype(jnp.float32))[..., None] * inverse
    cosine, sine = jnp.cos(angles), jnp.sin(angles)
    q = both[:, : slots * heads].reshape(shards, 2, slots // 2, heads, width)
    q = q.transpose(1, 3, 0, 2, 4).astype(jnp.float32)
    q = rotate(q, cosine[:, None], sine[:, None])
    tokens = shards * slots // 2
    q = q.reshape(2, heads * tokens, width)

    def new_rows(start):
        rows = both[:, start : start + slots].reshape(shards, 2, slots // 2, width)
        return rows.transpose(1, 0, 2, 3)

    new_k = rotate(new_rows(slots * heads).astype(jnp.float32), cosine, sine)
    new_k = new_k.reshape(2 * tokens, width)
    new_v = new_rows(slots * heads + slots).reshape(2 * tokens, width)
    kept = live & (jnp.arange(shards)[None, :, None] % 2 == core)
    key_index = jnp.where(kept, index.astype(jnp.float32), CLOSED).reshape(1, 2 * tokens)
    key_index = jnp.broadcast_to(key_index, (8, 2 * tokens))
    row_index = jnp.broadcast_to(
        index.astype(jnp.float32).reshape(2, 1, tokens, 1), (2, STEP // tokens, tokens, 128)
    ).reshape(2, STEP, 128)

    def plan(which):
        return jnp.concatenate([jnp.full((1,), which, jnp.int32), own_lens])

    start = plan(0)
    sums = attend(1, start, q, [dealt[0, 0]], None, (new_k, new_v, key_index, row_index), 2)
    at_len = 2
    for blocks in arrived[:-1]:
        sums = attend(at_len, start, q, blocks, sums, None, 2)
        at_len += len(blocks)
    (message,) = attend(at_len, plan(1 - core), q, arrived[-1], sums, None, 1, True, True)
    message = lax.ppermute(message, "core", other_core)
    sums, tail = attend(at_len, plan(core), q, arrived[-1], sums, None, 1, True)
    live_rows = lax.dynamic_index_in_dim(live, core, 0, keepdims=False)
    live_rows = live_rows.astype(jnp.float32).reshape(tokens, 1)
    attended = merge(sums, tail, message, jnp.broadcast_to(live_rows, (tokens, 128)))

    attended = attended.reshape(nheads, tokens // nheads, heads * width)
    up = [(i, (i + 1) % nz) for i in range(nz)]
    down = [(i, (i - 1) % nz) for i in range(nz)]
    held = {0: attended}
    for step in range(1, nz // 2):
        held[-step % nz] = lax.ppermute(held[(1 - step) % nz], "z", up)
        held[step] = lax.ppermute(held[step - 1], "z", down)
    def parts_of(which):
        rows = jnp.stack([held[k] for k in which], 1)
        rows = rows.reshape(-1, heads * width)
        parts = jnp.einsum("rk,wkn->wrn", rows, weights, preferred_element_type=jnp.float32)
        return parts.astype(jnp.bfloat16).reshape(4 * nheads, -1, out_weight.shape[1])

    early = (0, 1, 2, nz - 2, nz - 1)
    late = tuple(range(3, nz - 2))
    early_parts = parts_of(early)
    middle = nz // 2
    from_below, from_above, early_parts = lax.optimization_barrier(
        (held[middle + 1], held[middle - 1], early_parts)
    )
    cut = max(nheads // 2, 1)
    held[middle] = jnp.concatenate(
        [
            lax.ppermute(from_below[:cut], "z", up),
            lax.ppermute(from_above[cut:], "z", down),
        ],
        0,
    )
    parts = jnp.concatenate([early_parts, parts_of(late)], 1)
    got = lax.all_to_all(parts, ("y", "core", "head"), 0, 0, tiled=True)
    got = got.reshape(ny, 2, nheads, nz, tokens // nheads, -1)
    done = jnp.sum(got.astype(jnp.float32), 2).astype(jnp.bfloat16)
    order = early + late
    done = unroll(jnp.stack([done[:, :, order.index(k)] for k in range(nz)], 0), 0, z)
    done = done.reshape(nz, ny, 2, shards // nheads, slots // 2, -1)
    done = done.transpose(3, 1, 0, 2, 4, 5)
    return done.reshape(shards // nheads * convs * slots, -1)


def solution(mesh):
    blk, head = mesh.shape["blk"], mesh.shape["head"]
    fine = Mesh(mesh.devices.reshape(2, blk // 4, 2, head), ("y", "z", "core", "head"))
    blk = ("y", "z", "core")
    return jax.shard_map(
        body,
        mesh=fine,
        in_specs=(
            P(blk, "head", None),
            P(blk, "head", None),
            P(blk, "head", None),
            P(blk, None, "head", None, None),
            P(blk, None, "head", None, None),
            P(blk, None),
            P(),
            P(),
            P("head", blk),
        ),
        out_specs=P("head", blk),
        check_vma=False,
    )
```

```python
import functools

import jax
import jax.numpy as jnp
from jax import lax
from jax.experimental import pallas as pl
from jax.experimental.pallas import tpu as pltpu
from jax.sharding import Mesh, PartitionSpec as P

LOG2_E = 1.4426950408889634
CLOSED = 1.0e9
SHUT = -1.0e30
STEP = 256
LEGS = (
    ((0, 4), (0, 3), (0, -3)),
    ((0, 2), (0, -2), (0, 1), (0, -1)),
    ((1, 4), (1, 3), (1, -3), (1, 2)),
    ((1, -2), (1, 1), (1, -1), (1, 0)),
)


def deal_kernel(targets, at_ref, keys_ref, values_ref, *refs):
    outs, (stage, in_sems, out_sems) = refs[:-3], refs[-3:]
    ny, nz = targets[0]
    slots = keys_ref.shape[3]
    copies = []
    for i, (dy, dz) in enumerate(targets[1]):
        conversation = lax.rem(at_ref[0] + dy, ny) * nz + lax.rem(at_ref[1] + (dz + nz) % nz, nz)
        for j, ref in enumerate((keys_ref, values_ref)):
            copy = pltpu.make_async_copy(
                ref.at[0, conversation, 0], stage.at[i, pl.ds(j * slots, slots)], in_sems.at[i, j]
            )
            copy.start()
            copies.append(copy)
    leaving = []
    for i in range(len(outs)):
        copies[2 * i].wait()
        copies[2 * i + 1].wait()
        copy = pltpu.make_async_copy(stage.at[i], outs[i], out_sems.at[i])
        copy.start()
        leaving.append(copy)
    for copy in leaving:
        copy.wait()


def deal(at, keys, values, grid, targets):
    slots, width = keys.shape[3], keys.shape[4]
    anywhere = pl.BlockSpec(memory_space=pl.ANY)
    count = len(targets)
    return pl.pallas_call(
        functools.partial(deal_kernel, (grid, targets)),
        in_specs=[pl.BlockSpec(memory_space=pltpu.SMEM), anywhere, anywhere],
        out_specs=[anywhere] * count,
        out_shape=[jax.ShapeDtypeStruct((2 * slots, width), jnp.bfloat16)] * count,
        scratch_shapes=[
            pltpu.VMEM((count, 2 * slots, width), jnp.bfloat16),
            pltpu.SemaphoreType.DMA((count, 2)),
            pltpu.SemaphoreType.DMA((count,)),
        ],
    )(at, keys, values)


def attend_kernel(first_len, shards, first, role, plan_ref, q_ref, *refs):
    refs = list(refs)
    keys_ref, values_ref = refs[-2:]
    kv_refs = [refs.pop(0) for _ in range(shards)]
    if first:
        new_k_ref, new_v_ref, key_index_ref, row_index_ref = [refs.pop(0) for _ in range(4)]
    else:
        sums_ref = refs.pop(0)
    if role == "finish":
        message_ref, live_ref = refs.pop(0), refs.pop(0)
    out_ref = refs.pop(0)
    rows, width = q_ref.shape[1], q_ref.shape[2]
    slots = kv_refs[0].shape[0] // 2
    scale = LOG2_E / width**0.5

    @pl.when(pl.program_id(0) == 0)
    def _():
        first_lane = lax.broadcasted_iota(jnp.int32, (slots, width), 1) == 0
        slot = lax.broadcasted_iota(jnp.int32, (slots, width), 0)
        for i, ref in enumerate(kv_refs):
            at = slice(i * slots, (i + 1) * slots)
            keys_ref[at, 0:width] = ref[0:slots, :]
            shut = first_lane & (slot >= plan_ref[first_len + i])
            keys_ref[at, width : 2 * width] = jnp.where(shut, SHUT, 0.0).astype(jnp.bfloat16)
            values_ref[at, 0:width] = ref[slots : 2 * slots, :]
            values_ref[at, width : 2 * width] = jnp.ones((slots, width), jnp.bfloat16)

    lane = lax.broadcasted_iota(jnp.int32, (STEP, width), 1)
    unit = jnp.where(lane == 0, 1.0, 0.0).astype(jnp.bfloat16)
    if first:
        seen = key_index_ref[0:1, :] <= row_index_ref[0]
        ones = jnp.ones((new_v_ref.shape[0], width), jnp.bfloat16)

    if role == "finish":
        row = lax.broadcasted_iota(jnp.int32, (width, 2 * width), 0)
        group = jnp.where(lax.broadcasted_iota(jnp.int32, (width, 2 * width), 1) < width, 0, 3)
        spread = jnp.where((row >= group) & (row < group + 3), 1.0, 0.0).astype(jnp.bfloat16)

    def score(a, b):
        return lax.dot_general(a, b, (((1,), (1,)), ((), ())), preferred_element_type=jnp.float32)

    def scores(step):
        q = q_ref[0, step * STEP : (step + 1) * STEP, :]
        wide = jnp.concatenate([q, unit], 1)
        found = [score(wide, keys_ref[i * slots : (i + 1) * slots, :]) for i in range(shards)]
        if first:
            found.append(jnp.where(seen, score(q, new_k_ref[...]), SHUT))
        return found

    def highest(found, step):
        top = jnp.max(functools.reduce(jnp.maximum, found[:shards]), axis=1, keepdims=True)
        if first:
            return jnp.maximum(top, jnp.max(found[shards], axis=1, keepdims=True))
        before = sums_ref[0, step * STEP : (step + 1) * STEP, 2 * width - 1 : 2 * width]
        return jnp.maximum(top, before)

    steps = rows // STEP
    after = scores(0)
    after_top = highest(after, 0)
    for step in range(steps):
        at = slice(step * STEP, (step + 1) * STEP)
        found, top = after, after_top
        if step + 1 < steps:
            after = scores(step + 1)
        low = top * scale
        if first:
            sums = jnp.zeros((STEP, 2 * width), jnp.float32)
        else:
            sums = sums_ref[0, at, :]
            sums = sums * jnp.exp2(sums[:, 2 * width - 1 : 2 * width] * scale - low)
        for i, s in enumerate(found):
            w = jnp.exp2(s * scale - low).astype(jnp.bfloat16)
            if i < shards:
                v = values_ref[i * slots : (i + 1) * slots, :]
            else:
                v = jnp.concatenate([new_v_ref[...], ones], 1)
            sums = sums + jnp.dot(w, v, preferred_element_type=jnp.float32)
        if step + 1 < steps:
            after_top = highest(after, step + 1)
        if role == "message":
            tail = jnp.zeros((STEP, width), jnp.float32)
            total = sums[:, width : 2 * width]
            for i, value in enumerate((total, jnp.broadcast_to(top, total.shape))):
                for j in range(3):
                    part = value.astype(jnp.bfloat16).astype(jnp.float32)
                    tail = jnp.where(lane == 3 * i + j, part, tail)
                    value = value - part
            out_ref[at, 0:width] = sums[:, 0:width].astype(jnp.bfloat16)
            out_ref[at, width : 2 * width] = tail.astype(jnp.bfloat16)
        elif role == "finish":
            stats = jnp.dot(
                message_ref[at, width : 2 * width], spread, preferred_element_type=jnp.float32
            )
            highest_of_all = jnp.maximum(top, stats[:, width:])
            a = jnp.exp2((top - highest_of_all) * scale)
            b = jnp.exp2((stats[:, width:] - highest_of_all) * scale)
            total = sums[:, width : width + 1] * a + stats[:, :width] * b
            other = message_ref[at, 0:width].astype(jnp.float32)
            mixed = (sums[:, 0:width] * a + other * b) / total
            tokens = live_ref.shape[0]
            for i in range(STEP // tokens):
                head = step * (STEP // tokens) + i
                block = mixed[i * tokens : (i + 1) * tokens, :] * live_ref[...]
                out_ref[:, head * width : (head + 1) * width] = block.astype(jnp.bfloat16)
        else:
            out_ref[0, at, 0:width] = sums[:, 0:width]
            out_ref[0, at, width : 2 * width] = jnp.where(
                lane < width // 2, sums[:, width : 2 * width], top
            )


def attend(first_len, plan, q, kv, sums, new, halves, role="", more=()):
    both, rows, width = q.shape
    slots = kv[0].shape[0] // 2
    part = lambda *tail: pl.BlockSpec((1,) + tail, lambda i, s: (lax.rem(s[0] + i, both), 0, 0))
    whole = lambda a: pl.BlockSpec(a.shape, lambda i, s: (0,) * len(a.shape))
    in_specs = [part(rows, width)] + [whole(a) for a in kv]
    if sums is None:
        in_specs += [whole(a) for a in new[:3]] + [part(*new[3].shape[1:])]
        extra = tuple(new)
    else:
        in_specs.append(whole(sums) if sums.shape[0] == 1 else part(rows, 2 * width))
        extra = (sums,)
    in_specs += [whole(a) for a in more]
    if role == "message":
        out_shape = jax.ShapeDtypeStruct((rows, 2 * width), jnp.bfloat16)
        out_spec = whole(out_shape)
    elif role == "finish":
        tokens = more[1].shape[0]
        out_shape = jax.ShapeDtypeStruct((tokens, rows // tokens * width), jnp.bfloat16)
        out_spec = whole(out_shape)
    else:
        out_shape = jax.ShapeDtypeStruct((halves, rows, 2 * width), jnp.float32)
        out_spec = whole(out_shape) if halves == 1 else part(rows, 2 * width)
    wide = pltpu.VMEM((len(kv) * slots, 2 * width), jnp.bfloat16)
    keys = len(kv) * slots
    return pl.pallas_call(
        functools.partial(attend_kernel, first_len, len(kv), sums is None, role),
        grid_spec=pltpu.PrefetchScalarGridSpec(
            num_scalar_prefetch=1,
            grid=(halves,),
            in_specs=in_specs,
            out_specs=out_spec,
            scratch_shapes=[wide, wide],
        ),
        out_shape=out_shape,
        compiler_params=pltpu.CompilerParams(vmem_limit_bytes=40 * 1024 * 1024),
        cost_estimate=pl.CostEstimate(
            flops=16 * halves * rows * width * keys,
            bytes_accessed=halves * rows * width * 16,
            transcendentals=halves * rows * keys,
        ),
    )(plan, q, *kv, *extra, *more)


def rotate(values, cosine, sine):
    half = values.shape[-1] // 2
    first, second = values[..., :half], values[..., half:]
    return jnp.concatenate(
        [first * cosine - second * sine, second * cosine + first * sine], -1
    ).astype(jnp.bfloat16)


def body(
    queries,
    unrotated_key_rows,
    incoming_value_rows,
    cache_keys,
    stored_value_rows,
    cache_len,
    new_count,
    slot_index,
    out_weight,
):
    ny, nz, nheads = lax.axis_size("y"), lax.axis_size("z"), lax.axis_size("head")
    y, z, core = lax.axis_index("y"), lax.axis_index("z"), lax.axis_index("core")
    convs, slots = slot_index.shape[1], slot_index.shape[2]
    shards = slot_index.shape[0]
    heads, width = queries.shape[1], queries.shape[2]
    here = y * nz + z
    other_core = [(0, 1), (1, 0)]

    def unroll(values, axis, by):
        size = values.shape[axis]
        twice = jnp.concatenate([values, values], axis)
        return lax.dynamic_slice_in_dim(twice, (size - by) % size, size, axis)

    small = jnp.concatenate(
        [
            queries.reshape(convs, slots * heads, width),
            unrotated_key_rows.reshape(convs, slots, width),
            incoming_value_rows.reshape(convs, slots, width),
            jnp.broadcast_to(
                cache_len[0].astype(jnp.bfloat16)[:, None, None], (convs, 16 - 2 * slots, width)
            ),
        ],
        1,
    )
    mine = lax.all_to_all(small, ("y", "z"), 0, 0, tiled=True)
    theirs = lax.ppermute(mine, "core", other_core)

    targets = ((0, 0),) + tuple(leg for group in LEGS for leg in group)
    at = jnp.stack([y, z]).astype(jnp.int32)
    dealt = dict(zip(targets, deal(at, cache_keys, stored_value_rows, (ny, nz), targets)))

    def sent(dy, dz):
        route = [
            (a * nz + b, (a + dy) % ny * nz + (b + dz) % nz) for a in range(ny) for b in range(nz)
        ]
        return lax.ppermute(dealt[dy, dz], ("y", "z"), route)

    depth = out_weight.shape[0] // 2
    other_y = [(0, 1), (1, 0)]
    weight_y = [lax.ppermute(out_weight[:depth], "y", other_y)]
    arrived = []
    for i, group in enumerate(LEGS):
        if i == 2:
            late_legs = [leg for some in LEGS[2:] for leg in some]
            held_back = lax.optimization_barrier(
                tuple(dealt[leg] for leg in late_legs) + (weight_y[0],)
            )
            weight_y[0] = held_back[-1]
            dealt.update(zip(late_legs, held_back))
        arrived.append([sent(*leg) for leg in group])
    rest, _ = lax.optimization_barrier((out_weight[depth:], arrived[-1][-1]))
    weight_y.append(lax.ppermute(rest, "y", other_y))
    core_part, _ = lax.optimization_barrier((out_weight, arrived[0][0]))
    weight_core = lax.ppermute(core_part, "core", other_core)

    both = jnp.where(core == 0, jnp.stack([mine, theirs], 1), jnp.stack([theirs, mine], 1))
    both = both.reshape(shards, small.shape[1], width)
    base = jnp.sum(both[:, slots * heads + 2 * slots, 0].astype(jnp.float32))
    own_lens = mine[:, slots * heads + 2 * slots, 0].astype(jnp.int32)
    senders = [(y - dy) % ny * nz + (z - dz) % nz for dy, dz in targets]
    own_lens = jnp.sum(
        jnp.where(jnp.stack(senders)[:, None] == jnp.arange(convs), own_lens[None, :], 0), 1
    )
    index = lax.dynamic_index_in_dim(slot_index, here, 1, keepdims=False)
    index = index.reshape(shards, 2, slots // 2).transpose(1, 0, 2)
    live = index < new_count[here]
    inverse = 1.0 / 500000.0 ** (jnp.arange(0, width, 2, dtype=jnp.float32) / width)
    angles = (base + index.astype(jnp.float32))[..., None] * inverse
    cosine, sine = jnp.cos(angles), jnp.sin(angles)
    q = both[:, : slots * heads].reshape(shards, 2, slots // 2, heads, width)
    q = q.transpose(1, 3, 0, 2, 4).astype(jnp.float32)
    q = rotate(q, cosine[:, None], sine[:, None])
    tokens = shards * slots // 2
    q = q.reshape(2, heads * tokens, width)

    def new_rows(start):
        rows = both[:, start : start + slots].reshape(shards, 2, slots // 2, width)
        return rows.transpose(1, 0, 2, 3)

    new_k = rotate(new_rows(slots * heads).astype(jnp.float32), cosine, sine)
    new_k = new_k.reshape(2 * tokens, width)
    new_v = new_rows(slots * heads + slots).reshape(2 * tokens, width)
    kept = live & (jnp.arange(shards)[None, :, None] % 2 == core)
    key_index = jnp.where(kept, index.astype(jnp.float32), CLOSED).reshape(1, 2 * tokens)
    key_index = jnp.broadcast_to(key_index, (8, 2 * tokens))
    row_index = jnp.broadcast_to(
        index.astype(jnp.float32).reshape(2, 1, tokens, 1), (2, STEP // tokens, tokens, 128)
    ).reshape(2, STEP, 128)

    def plan(which):
        return jnp.concatenate([jnp.full((1,), which, jnp.int32), own_lens])

    start = plan(0)
    sums = attend(1, start, q, [dealt[0, 0]], None, (new_k, new_v, key_index, row_index), 2)
    at_len = 2
    for blocks in arrived[:-2]:
        sums = attend(at_len, start, q, blocks, sums, None, 2)
        at_len += len(blocks)
    ours, others = plan(core), plan(1 - core)
    last_len = at_len + len(arrived[-2])
    message = attend(at_len, others, q, arrived[-2], sums, None, 1)
    message = attend(last_len, others, q, arrived[-1], message, None, 1, "message")
    message = lax.ppermute(message, "core", other_core)
    live_rows = lax.dynamic_index_in_dim(live, core, 0, keepdims=False)
    live_rows = jnp.broadcast_to(live_rows.astype(jnp.float32).reshape(tokens, 1), (tokens, 128))
    sums = attend(at_len, ours, q, arrived[-2], sums, None, 1)
    attended = attend(
        last_len, ours, q, arrived[-1], sums, None, 1, "finish", (message, live_rows)
    )

    attended = attended.reshape(nheads, tokens // nheads, heads * width)
    up = [(i, (i + 1) % nz) for i in range(nz)]
    down = [(i, (i - 1) % nz) for i in range(nz)]
    held = {0: attended}
    for step in range(1, nz // 2):
        held[-step % nz] = lax.ppermute(held[(1 - step) % nz], "z", up)
        held[step] = lax.ppermute(held[step - 1], "z", down)
    first_half, _ = lax.optimization_barrier((weight_y[0], attended))
    second_half, _ = lax.optimization_barrier((weight_y[1], held[2]))
    weight_far = jnp.concatenate([first_half, second_half], 0)
    weight_both = jnp.concatenate(
        [
            lax.ppermute(first_half, "core", other_core),
            lax.ppermute(second_half, "core", other_core),
        ],
        0,
    )
    near = [
        jnp.where(core == 0, out_weight, weight_core),
        jnp.where(core == 0, weight_core, out_weight),
    ]
    far = [
        jnp.where(core == 0, weight_far, weight_both),
        jnp.where(core == 0, weight_both, weight_far),
    ]
    weights = jnp.stack(
        [jnp.where(y == 0, a, b) for a, b in zip(near, far)]
        + [jnp.where(y == 0, b, a) for a, b in zip(near, far)]
    )

    def parts_of(which):
        rows = jnp.stack([held[k] for k in which], 1)
        rows = rows.reshape(-1, heads * width)
        parts = jnp.einsum("rk,wkn->wrn", rows, weights, preferred_element_type=jnp.float32)
        return parts.astype(jnp.bfloat16).reshape(4 * nheads, -1, out_weight.shape[1])

    early = (0, 1, 2, nz - 2, nz - 1)
    late = tuple(range(3, nz - 2))
    early_parts = parts_of(early)
    middle = nz // 2
    from_below, from_above, early_parts = lax.optimization_barrier(
        (held[middle + 1], held[middle - 1], early_parts)
    )
    cut = max(nheads // 2, 1)
    held[middle] = jnp.concatenate(
        [
            lax.ppermute(from_below[:cut], "z", up),
            lax.ppermute(from_above[cut:], "z", down),
        ],
        0,
    )
    parts = jnp.concatenate([early_parts, parts_of(late)], 1)
    got = lax.all_to_all(parts, ("y", "core", "head"), 0, 0, tiled=True)
    got = got.reshape(ny, 2, nheads, nz, tokens // nheads, -1)
    done = jnp.sum(got.astype(jnp.float32), 2).astype(jnp.bfloat16)
    order = early + late
    done = unroll(jnp.stack([done[:, :, order.index(k)] for k in range(nz)], 0), 0, z)
    done = done.reshape(nz, ny, 2, shards // nheads, slots // 2, -1)
    done = done.transpose(3, 1, 0, 2, 4, 5)
    return done.reshape(shards // nheads * convs * slots, -1)


def solution(mesh):
    blk, head = mesh.shape["blk"], mesh.shape["head"]
    fine = Mesh(mesh.devices.reshape(2, blk // 4, 2, head), ("y", "z", "core", "head"))
    blk = ("y", "z", "core")
    return jax.shard_map(
        body,
        mesh=fine,
        in_specs=(
            P(blk, "head", None),
            P(blk, "head", None),
            P(blk, "head", None),
            P(blk, None, "head", None, None),
            P(blk, None, "head", None, None),
            P(blk, None),
            P(),
            P(),
            P("head", blk),
        ),
        out_specs=P("head", blk),
        check_vma=False,
    )
```

```python
import functools

import jax
import jax.numpy as jnp
from jax import lax
from jax.experimental import pallas as pl
from jax.experimental.pallas import tpu as pltpu
from jax.sharding import Mesh, PartitionSpec as P

LOG2_E = 1.4426950408889634
CLOSED = 1.0e9
SHUT = -1.0e30
STEP = 256
LEGS = (
    ((0, 1), (0, 4), (0, 3), (0, -3)),
    ((0, 2), (0, -2), (0, -1)),
    ((1, 4), (1, 3), (1, -3), (1, 2)),
    ((1, -2), (1, 1), (1, -1), (1, 0)),
)


def deal_kernel(targets, at_ref, keys_ref, values_ref, *refs):
    outs, (stage, in_sems, out_sems) = refs[:-3], refs[-3:]
    ny, nz = targets[0]
    slots = keys_ref.shape[3]
    copies = []
    for i, (dy, dz) in enumerate(targets[1]):
        conversation = lax.rem(at_ref[0] + dy, ny) * nz + lax.rem(at_ref[1] + (dz + nz) % nz, nz)
        for j, ref in enumerate((keys_ref, values_ref)):
            copy = pltpu.make_async_copy(
                ref.at[0, conversation, 0], stage.at[i, pl.ds(j * slots, slots)], in_sems.at[i, j]
            )
            copy.start()
            copies.append(copy)
    leaving = []
    for i in range(len(outs)):
        copies[2 * i].wait()
        copies[2 * i + 1].wait()
        copy = pltpu.make_async_copy(stage.at[i], outs[i], out_sems.at[i])
        copy.start()
        leaving.append(copy)
    for copy in leaving:
        copy.wait()


def deal(at, keys, values, grid, targets):
    slots, width = keys.shape[3], keys.shape[4]
    anywhere = pl.BlockSpec(memory_space=pl.ANY)
    count = len(targets)
    return pl.pallas_call(
        functools.partial(deal_kernel, (grid, targets)),
        in_specs=[pl.BlockSpec(memory_space=pltpu.SMEM), anywhere, anywhere],
        out_specs=[anywhere] * count,
        out_shape=[jax.ShapeDtypeStruct((2 * slots, width), jnp.bfloat16)] * count,
        scratch_shapes=[
            pltpu.VMEM((count, 2 * slots, width), jnp.bfloat16),
            pltpu.SemaphoreType.DMA((count, 2)),
            pltpu.SemaphoreType.DMA((count,)),
        ],
    )(at, keys, values)


def attend_kernel(first_len, shards, first, role, plan_ref, q_ref, *refs):
    refs = list(refs)
    keys_ref, values_ref = refs[-2:]
    kv_refs = [refs.pop(0) for _ in range(shards)]
    if first:
        new_k_ref, new_v_ref, key_index_ref, row_index_ref = [refs.pop(0) for _ in range(4)]
    else:
        sums_ref = refs.pop(0)
    if role == "finish":
        message_ref, live_ref = refs.pop(0), refs.pop(0)
    out_ref = refs.pop(0)
    rows, width = q_ref.shape[1], q_ref.shape[2]
    slots = kv_refs[0].shape[0] // 2
    scale = LOG2_E / width**0.5

    @pl.when(pl.program_id(0) == 0)
    def _():
        first_lane = lax.broadcasted_iota(jnp.int32, (slots, width), 1) == 0
        slot = lax.broadcasted_iota(jnp.int32, (slots, width), 0)
        for i, ref in enumerate(kv_refs):
            at = slice(i * slots, (i + 1) * slots)
            keys_ref[at, 0:width] = ref[0:slots, :]
            shut = first_lane & (slot >= plan_ref[first_len + i])
            keys_ref[at, width : 2 * width] = jnp.where(shut, SHUT, 0.0).astype(jnp.bfloat16)
            values_ref[at, 0:width] = ref[slots : 2 * slots, :]
            values_ref[at, width : 2 * width] = jnp.ones((slots, width), jnp.bfloat16)

    lane = lax.broadcasted_iota(jnp.int32, (STEP, width), 1)
    unit = jnp.where(lane == 0, 1.0, 0.0).astype(jnp.bfloat16)
    if first:
        seen = key_index_ref[0:1, :] <= row_index_ref[0]
        ones = jnp.ones((new_v_ref.shape[0], width), jnp.bfloat16)

    if role == "finish":
        row = lax.broadcasted_iota(jnp.int32, (width, 2 * width), 0)
        group = jnp.where(lax.broadcasted_iota(jnp.int32, (width, 2 * width), 1) < width, 0, 3)
        spread = jnp.where((row >= group) & (row < group + 3), 1.0, 0.0).astype(jnp.bfloat16)

    def score(a, b):
        return lax.dot_general(a, b, (((1,), (1,)), ((), ())), preferred_element_type=jnp.float32)

    def scores(step):
        q = q_ref[0, step * STEP : (step + 1) * STEP, :]
        wide = jnp.concatenate([q, unit], 1)
        found = [score(wide, keys_ref[i * slots : (i + 1) * slots, :]) for i in range(shards)]
        if first:
            found.append(jnp.where(seen, score(q, new_k_ref[...]), SHUT))
        return found

    def highest(found, step):
        top = jnp.max(functools.reduce(jnp.maximum, found[:shards]), axis=1, keepdims=True)
        if first:
            return jnp.maximum(top, jnp.max(found[shards], axis=1, keepdims=True))
        before = sums_ref[0, step * STEP : (step + 1) * STEP, 2 * width - 1 : 2 * width]
        return jnp.maximum(top, before)

    steps = rows // STEP
    after = scores(0)
    after_top = highest(after, 0)
    for step in range(steps):
        at = slice(step * STEP, (step + 1) * STEP)
        found, top = after, after_top
        if step + 1 < steps:
            after = scores(step + 1)
        low = top * scale
        if first:
            sums = jnp.zeros((STEP, 2 * width), jnp.float32)
        else:
            sums = sums_ref[0, at, :]
            sums = sums * jnp.exp2(sums[:, 2 * width - 1 : 2 * width] * scale - low)
        for i, s in enumerate(found):
            w = jnp.exp2(s * scale - low).astype(jnp.bfloat16)
            if i < shards:
                v = values_ref[i * slots : (i + 1) * slots, :]
            else:
                v = jnp.concatenate([new_v_ref[...], ones], 1)
            sums = sums + jnp.dot(w, v, preferred_element_type=jnp.float32)
        if step + 1 < steps:
            after_top = highest(after, step + 1)
        if role == "message":
            tail = jnp.zeros((STEP, width), jnp.float32)
            total = sums[:, width : 2 * width]
            for i, value in enumerate((total, jnp.broadcast_to(top, total.shape))):
                for j in range(3):
                    part = value.astype(jnp.bfloat16).astype(jnp.float32)
                    tail = jnp.where(lane == 3 * i + j, part, tail)
                    value = value - part
            out_ref[at, 0:width] = sums[:, 0:width].astype(jnp.bfloat16)
            out_ref[at, width : 2 * width] = tail.astype(jnp.bfloat16)
        elif role == "finish":
            stats = jnp.dot(
                message_ref[at, width : 2 * width], spread, preferred_element_type=jnp.float32
            )
            highest_of_all = jnp.maximum(top, stats[:, width:])
            a = jnp.exp2((top - highest_of_all) * scale)
            b = jnp.exp2((stats[:, width:] - highest_of_all) * scale)
            total = sums[:, width : width + 1] * a + stats[:, :width] * b
            other = message_ref[at, 0:width].astype(jnp.float32)
            mixed = (sums[:, 0:width] * a + other * b) / total
            tokens = live_ref.shape[0]
            for i in range(STEP // tokens):
                head = step * (STEP // tokens) + i
                block = mixed[i * tokens : (i + 1) * tokens, :] * live_ref[...]
                out_ref[:, head * width : (head + 1) * width] = block.astype(jnp.bfloat16)
        else:
            out_ref[0, at, 0:width] = sums[:, 0:width]
            out_ref[0, at, width : 2 * width] = jnp.where(
                lane < width // 2, sums[:, width : 2 * width], top
            )


def attend(first_len, plan, q, kv, sums, new, halves, role="", more=()):
    both, rows, width = q.shape
    slots = kv[0].shape[0] // 2
    part = lambda *tail: pl.BlockSpec((1,) + tail, lambda i, s: (lax.rem(s[0] + i, both), 0, 0))
    whole = lambda a: pl.BlockSpec(a.shape, lambda i, s: (0,) * len(a.shape))
    in_specs = [part(rows, width)] + [whole(a) for a in kv]
    if sums is None:
        in_specs += [whole(a) for a in new[:3]] + [part(*new[3].shape[1:])]
        extra = tuple(new)
    else:
        in_specs.append(whole(sums) if sums.shape[0] == 1 else part(rows, 2 * width))
        extra = (sums,)
    in_specs += [whole(a) for a in more]
    if role == "message":
        out_shape = jax.ShapeDtypeStruct((rows, 2 * width), jnp.bfloat16)
        out_spec = whole(out_shape)
    elif role == "finish":
        tokens = more[1].shape[0]
        out_shape = jax.ShapeDtypeStruct((tokens, rows // tokens * width), jnp.bfloat16)
        out_spec = whole(out_shape)
    else:
        out_shape = jax.ShapeDtypeStruct((halves, rows, 2 * width), jnp.float32)
        out_spec = whole(out_shape) if halves == 1 else part(rows, 2 * width)
    wide = pltpu.VMEM((len(kv) * slots, 2 * width), jnp.bfloat16)
    keys = len(kv) * slots
    return pl.pallas_call(
        functools.partial(attend_kernel, first_len, len(kv), sums is None, role),
        grid_spec=pltpu.PrefetchScalarGridSpec(
            num_scalar_prefetch=1,
            grid=(halves,),
            in_specs=in_specs,
            out_specs=out_spec,
            scratch_shapes=[wide, wide],
        ),
        out_shape=out_shape,
        compiler_params=pltpu.CompilerParams(vmem_limit_bytes=40 * 1024 * 1024),
        cost_estimate=pl.CostEstimate(
            flops=16 * halves * rows * width * keys,
            bytes_accessed=halves * rows * width * 16,
            transcendentals=halves * rows * keys,
        ),
    )(plan, q, *kv, *extra, *more)


def rotate(values, cosine, sine):
    half = values.shape[-1] // 2
    first, second = values[..., :half], values[..., half:]
    return jnp.concatenate(
        [first * cosine - second * sine, second * cosine + first * sine], -1
    ).astype(jnp.bfloat16)


def body(
    queries,
    unrotated_key_rows,
    incoming_value_rows,
    cache_keys,
    stored_value_rows,
    cache_len,
    new_count,
    slot_index,
    out_weight,
):
    ny, nz, nheads = lax.axis_size("y"), lax.axis_size("z"), lax.axis_size("head")
    y, z, core = lax.axis_index("y"), lax.axis_index("z"), lax.axis_index("core")
    convs, slots = slot_index.shape[1], slot_index.shape[2]
    shards = slot_index.shape[0]
    heads, width = queries.shape[1], queries.shape[2]
    here = y * nz + z
    other_core = [(0, 1), (1, 0)]

    def unroll(values, axis, by):
        size = values.shape[axis]
        twice = jnp.concatenate([values, values], axis)
        return lax.dynamic_slice_in_dim(twice, (size - by) % size, size, axis)

    small = jnp.concatenate(
        [
            queries.reshape(convs, slots * heads, width),
            unrotated_key_rows.reshape(convs, slots, width),
            incoming_value_rows.reshape(convs, slots, width),
            jnp.broadcast_to(
                cache_len[0].astype(jnp.bfloat16)[:, None, None], (convs, 16 - 2 * slots, width)
            ),
        ],
        1,
    )
    targets = ((0, 0),) + tuple(leg for group in LEGS for leg in group)
    at = jnp.stack([y, z]).astype(jnp.int32)
    dealt = dict(zip(targets, deal(at, cache_keys, stored_value_rows, (ny, nz), targets)))

    def sent(dy, dz):
        route = [
            (a * nz + b, (a + dy) % ny * nz + (b + dz) % nz) for a in range(ny) for b in range(nz)
        ]
        return lax.ppermute(dealt[dy, dz], ("y", "z"), route)

    depth = out_weight.shape[0] // 2
    other_y = [(0, 1), (1, 0)]
    weight_y = [lax.ppermute(out_weight[:depth], "y", other_y)]
    arrived = [[sent(*leg) for leg in LEGS[0]]]
    small, arrived[0][0] = lax.optimization_barrier((small, arrived[0][0]))
    mine = lax.all_to_all(small, ("y", "z"), 0, 0, tiled=True)
    joined = lax.optimization_barrier((mine, weight_y[0], *arrived[0]))
    mine, weight_y[0], arrived[0] = joined[0], joined[1], list(joined[2:])
    theirs = lax.ppermute(mine, "core", other_core)
    late_legs = [leg for group in LEGS[1:] for leg in group]
    held_back = lax.optimization_barrier(
        tuple(dealt[leg] for leg in late_legs) + (weight_y[0],)
    )
    weight_y[0] = held_back[-1]
    dealt.update(zip(late_legs, held_back))
    arrived += [[sent(*leg) for leg in group] for group in LEGS[1:]]
    rest, _ = lax.optimization_barrier((out_weight[depth:], arrived[-1][-1]))
    weight_y.append(lax.ppermute(rest, "y", other_y))
    core_part, _ = lax.optimization_barrier((out_weight, arrived[0][0]))
    weight_core = lax.ppermute(core_part, "core", other_core)

    both = jnp.where(core == 0, jnp.stack([mine, theirs], 1), jnp.stack([theirs, mine], 1))
    both = both.reshape(shards, small.shape[1], width)
    base = jnp.sum(both[:, slots * heads + 2 * slots, 0].astype(jnp.float32))
    own_lens = mine[:, slots * heads + 2 * slots, 0].astype(jnp.int32)
    senders = [(y - dy) % ny * nz + (z - dz) % nz for dy, dz in targets]
    own_lens = jnp.sum(
        jnp.where(jnp.stack(senders)[:, None] == jnp.arange(convs), own_lens[None, :], 0), 1
    )
    index = lax.dynamic_index_in_dim(slot_index, here, 1, keepdims=False)
    index = index.reshape(shards, 2, slots // 2).transpose(1, 0, 2)
    live = index < new_count[here]
    inverse = 1.0 / 500000.0 ** (jnp.arange(0, width, 2, dtype=jnp.float32) / width)
    angles = (base + index.astype(jnp.float32))[..., None] * inverse
    cosine, sine = jnp.cos(angles), jnp.sin(angles)
    q = both[:, : slots * heads].reshape(shards, 2, slots // 2, heads, width)
    q = q.transpose(1, 3, 0, 2, 4).astype(jnp.float32)
    q = rotate(q, cosine[:, None], sine[:, None])
    tokens = shards * slots // 2
    q = q.reshape(2, heads * tokens, width)

    def new_rows(start):
        rows = both[:, start : start + slots].reshape(shards, 2, slots // 2, width)
        return rows.transpose(1, 0, 2, 3)

    new_k = rotate(new_rows(slots * heads).astype(jnp.float32), cosine, sine)
    new_k = new_k.reshape(2 * tokens, width)
    new_v = new_rows(slots * heads + slots).reshape(2 * tokens, width)
    kept = live & (jnp.arange(shards)[None, :, None] % 2 == core)
    key_index = jnp.where(kept, index.astype(jnp.float32), CLOSED).reshape(1, 2 * tokens)
    key_index = jnp.broadcast_to(key_index, (8, 2 * tokens))
    row_index = jnp.broadcast_to(
        index.astype(jnp.float32).reshape(2, 1, tokens, 1), (2, STEP // tokens, tokens, 128)
    ).reshape(2, STEP, 128)

    def plan(which):
        return jnp.concatenate([jnp.full((1,), which, jnp.int32), own_lens])

    start = plan(0)
    sums = attend(1, start, q, [dealt[0, 0]], None, (new_k, new_v, key_index, row_index), 2)
    at_len = 2
    for blocks in arrived[:-2]:
        sums = attend(at_len, start, q, blocks, sums, None, 2)
        at_len += len(blocks)
    ours, others = plan(core), plan(1 - core)
    last_len = at_len + len(arrived[-2])
    message = attend(at_len, others, q, arrived[-2], sums, None, 1)
    message = attend(last_len, others, q, arrived[-1], message, None, 1, "message")
    message = lax.ppermute(message, "core", other_core)
    live_rows = lax.dynamic_index_in_dim(live, core, 0, keepdims=False)
    live_rows = jnp.broadcast_to(live_rows.astype(jnp.float32).reshape(tokens, 1), (tokens, 128))
    sums = attend(at_len, ours, q, arrived[-2], sums, None, 1)
    attended = attend(
        last_len, ours, q, arrived[-1], sums, None, 1, "finish", (message, live_rows)
    )

    attended = attended.reshape(nheads, tokens // nheads, heads * width)
    up = [(i, (i + 1) % nz) for i in range(nz)]
    down = [(i, (i - 1) % nz) for i in range(nz)]
    held = {0: attended}
    for step in range(1, nz // 2):
        held[-step % nz] = lax.ppermute(held[(1 - step) % nz], "z", up)
        held[step] = lax.ppermute(held[step - 1], "z", down)
    first_half, _ = lax.optimization_barrier((weight_y[0], attended))
    second_half, _ = lax.optimization_barrier((weight_y[1], held[2]))
    weight_far = jnp.concatenate([first_half, second_half], 0)
    weight_both = jnp.concatenate(
        [
            lax.ppermute(first_half, "core", other_core),
            lax.ppermute(second_half, "core", other_core),
        ],
        0,
    )
    near = [
        jnp.where(core == 0, out_weight, weight_core),
        jnp.where(core == 0, weight_core, out_weight),
    ]
    far = [
        jnp.where(core == 0, weight_far, weight_both),
        jnp.where(core == 0, weight_both, weight_far),
    ]
    weights = jnp.stack(
        [jnp.where(y == 0, a, b) for a, b in zip(near, far)]
        + [jnp.where(y == 0, b, a) for a, b in zip(near, far)]
    )

    def parts_of(which):
        rows = jnp.stack([held[k] for k in which], 1)
        rows = rows.reshape(-1, heads * width)
        parts = jnp.einsum("rk,wkn->wrn", rows, weights, preferred_element_type=jnp.float32)
        return parts.astype(jnp.bfloat16).reshape(4 * nheads, -1, out_weight.shape[1])

    early = (0, 1, 2, nz - 2, nz - 1)
    late = tuple(range(3, nz - 2))
    early_parts = parts_of(early)
    middle = nz // 2
    from_below, from_above, early_parts = lax.optimization_barrier(
        (held[middle + 1], held[middle - 1], early_parts)
    )
    cut = max(nheads // 2, 1)
    held[middle] = jnp.concatenate(
        [
            lax.ppermute(from_below[:cut], "z", up),
            lax.ppermute(from_above[cut:], "z", down),
        ],
        0,
    )
    parts = jnp.concatenate([early_parts, parts_of(late)], 1)
    got = lax.all_to_all(parts, ("y", "core", "head"), 0, 0, tiled=True)
    got = got.reshape(ny, 2, nheads, nz, tokens // nheads, -1)
    done = jnp.sum(got.astype(jnp.float32), 2).astype(jnp.bfloat16)
    order = early + late
    done = unroll(jnp.stack([done[:, :, order.index(k)] for k in range(nz)], 0), 0, z)
    done = done.reshape(nz, ny, 2, shards // nheads, slots // 2, -1)
    done = done.transpose(3, 1, 0, 2, 4, 5)
    return done.reshape(shards // nheads * convs * slots, -1)


def solution(mesh):
    blk, head = mesh.shape["blk"], mesh.shape["head"]
    fine = Mesh(mesh.devices.reshape(2, blk // 4, 2, head), ("y", "z", "core", "head"))
    blk = ("y", "z", "core")
    return jax.shard_map(
        body,
        mesh=fine,
        in_specs=(
            P(blk, "head", None),
            P(blk, "head", None),
            P(blk, "head", None),
            P(blk, None, "head", None, None),
            P(blk, None, "head", None, None),
            P(blk, None),
            P(),
            P(),
            P("head", blk),
        ),
        out_specs=P("head", blk),
        check_vma=False,
    )
```

```python
import functools

import jax
import jax.numpy as jnp
from jax import lax
from jax.experimental import pallas as pl
from jax.experimental.pallas import tpu as pltpu
from jax.sharding import Mesh, PartitionSpec as P

LOG2_E = 1.4426950408889634
CLOSED = 1.0e9
SHUT = -1.0e30
STEP = 256
LEGS = (
    ((0, 1), (0, 4), (0, 3), (0, -3)),
    ((0, 2), (0, -2), (0, -1)),
    ((1, 4), (1, 3), (1, -3), (1, 2)),
    ((1, -2), (1, 1), (1, -1), (1, 0)),
)


def deal_kernel(targets, at_ref, keys_ref, values_ref, *refs):
    outs, (stage, in_sems, out_sems) = refs[:-3], refs[-3:]
    ny, nz = targets[0]
    slots = keys_ref.shape[3]
    copies = []
    for i, (dy, dz) in enumerate(targets[1]):
        conversation = lax.rem(at_ref[0] + dy, ny) * nz + lax.rem(at_ref[1] + (dz + nz) % nz, nz)
        for j, ref in enumerate((keys_ref, values_ref)):
            copy = pltpu.make_async_copy(
                ref.at[0, conversation, 0], stage.at[i, pl.ds(j * slots, slots)], in_sems.at[i, j]
            )
            copy.start()
            copies.append(copy)
    leaving = []
    for i in range(len(outs)):
        copies[2 * i].wait()
        copies[2 * i + 1].wait()
        copy = pltpu.make_async_copy(stage.at[i], outs[i], out_sems.at[i])
        copy.start()
        leaving.append(copy)
    for copy in leaving:
        copy.wait()


def deal(at, keys, values, grid, targets):
    slots, width = keys.shape[3], keys.shape[4]
    anywhere = pl.BlockSpec(memory_space=pl.ANY)
    count = len(targets)
    return pl.pallas_call(
        functools.partial(deal_kernel, (grid, targets)),
        in_specs=[pl.BlockSpec(memory_space=pltpu.SMEM), anywhere, anywhere],
        out_specs=[anywhere] * count,
        out_shape=[jax.ShapeDtypeStruct((2 * slots, width), jnp.bfloat16)] * count,
        scratch_shapes=[
            pltpu.VMEM((count, 2 * slots, width), jnp.bfloat16),
            pltpu.SemaphoreType.DMA((count, 2)),
            pltpu.SemaphoreType.DMA((count,)),
        ],
    )(at, keys, values)


def attend_kernel(first_len, shards, first, role, plan_ref, q_ref, *refs):
    refs = list(refs)
    keys_ref, values_ref = refs[-2:]
    kv_refs = [refs.pop(0) for _ in range(shards)]
    if first:
        new_k_ref, new_v_ref, key_index_ref, row_index_ref = [refs.pop(0) for _ in range(4)]
    else:
        sums_ref = refs.pop(0)
    if role == "finish":
        message_ref, live_ref = refs.pop(0), refs.pop(0)
    out_ref = refs.pop(0)
    rows, width = q_ref.shape[1], q_ref.shape[2]
    slots = kv_refs[0].shape[0] // 2
    scale = LOG2_E / width**0.5

    @pl.when(pl.program_id(0) == 0)
    def _():
        first_lane = lax.broadcasted_iota(jnp.int32, (slots, width), 1) == 0
        slot = lax.broadcasted_iota(jnp.int32, (slots, width), 0)
        for i, ref in enumerate(kv_refs):
            at = slice(i * slots, (i + 1) * slots)
            keys_ref[at, 0:width] = ref[0:slots, :]
            shut = first_lane & (slot >= plan_ref[first_len + i])
            keys_ref[at, width : 2 * width] = jnp.where(shut, SHUT, 0.0).astype(jnp.bfloat16)
            values_ref[at, 0:width] = ref[slots : 2 * slots, :]
            values_ref[at, width : 2 * width] = jnp.ones((slots, width), jnp.bfloat16)

    lane = lax.broadcasted_iota(jnp.int32, (STEP, width), 1)
    unit = jnp.where(lane == 0, 1.0, 0.0).astype(jnp.bfloat16)
    if first:
        seen = key_index_ref[0:1, :] <= row_index_ref[0]
        ones = jnp.ones((new_v_ref.shape[0], width), jnp.bfloat16)

    if role == "finish":
        row = lax.broadcasted_iota(jnp.int32, (width, 2 * width), 0)
        group = jnp.where(lax.broadcasted_iota(jnp.int32, (width, 2 * width), 1) < width, 0, 3)
        spread = jnp.where((row >= group) & (row < group + 3), 1.0, 0.0).astype(jnp.bfloat16)

    def score(a, b):
        return lax.dot_general(a, b, (((1,), (1,)), ((), ())), preferred_element_type=jnp.float32)

    def scores(step):
        q = q_ref[0, step * STEP : (step + 1) * STEP, :]
        wide = jnp.concatenate([q, unit], 1)
        found = [score(wide, keys_ref[i * slots : (i + 1) * slots, :]) for i in range(shards)]
        if first:
            found.append(jnp.where(seen, score(q, new_k_ref[...]), SHUT))
        return found

    def highest(found, step):
        top = jnp.max(functools.reduce(jnp.maximum, found[:shards]), axis=1, keepdims=True)
        if first:
            return jnp.maximum(top, jnp.max(found[shards], axis=1, keepdims=True))
        before = sums_ref[0, step * STEP : (step + 1) * STEP, 2 * width - 1 : 2 * width]
        return jnp.maximum(top, before)

    steps = rows // STEP
    after = scores(0)
    after_top = highest(after, 0)
    for step in range(steps):
        at = slice(step * STEP, (step + 1) * STEP)
        found, top = after, after_top
        if step + 1 < steps:
            after = scores(step + 1)
        low = top * scale
        if first:
            sums = jnp.zeros((STEP, 2 * width), jnp.float32)
        else:
            sums = sums_ref[0, at, :]
            sums = sums * jnp.exp2(sums[:, 2 * width - 1 : 2 * width] * scale - low)
        for i, s in enumerate(found):
            w = jnp.exp2(s * scale - low).astype(jnp.bfloat16)
            if i < shards:
                v = values_ref[i * slots : (i + 1) * slots, :]
            else:
                v = jnp.concatenate([new_v_ref[...], ones], 1)
            sums = sums + jnp.dot(w, v, preferred_element_type=jnp.float32)
        if step + 1 < steps:
            after_top = highest(after, step + 1)
        if role == "message":
            tail = jnp.zeros((STEP, width), jnp.float32)
            total = sums[:, width : 2 * width]
            for i, value in enumerate((total, jnp.broadcast_to(top, total.shape))):
                for j in range(3):
                    part = value.astype(jnp.bfloat16).astype(jnp.float32)
                    tail = jnp.where(lane == 3 * i + j, part, tail)
                    value = value - part
            out_ref[at, 0:width] = sums[:, 0:width].astype(jnp.bfloat16)
            out_ref[at, width : 2 * width] = tail.astype(jnp.bfloat16)
        elif role == "finish":
            stats = jnp.dot(
                message_ref[at, width : 2 * width], spread, preferred_element_type=jnp.float32
            )
            highest_of_all = jnp.maximum(top, stats[:, width:])
            a = jnp.exp2((top - highest_of_all) * scale)
            b = jnp.exp2((stats[:, width:] - highest_of_all) * scale)
            total = sums[:, width : width + 1] * a + stats[:, :width] * b
            other = message_ref[at, 0:width].astype(jnp.float32)
            mixed = (sums[:, 0:width] * a + other * b) / total
            tokens = live_ref.shape[0]
            for i in range(STEP // tokens):
                head = step * (STEP // tokens) + i
                block = mixed[i * tokens : (i + 1) * tokens, :] * live_ref[...]
                out_ref[:, head * width : (head + 1) * width] = block.astype(jnp.bfloat16)
        else:
            out_ref[0, at, 0:width] = sums[:, 0:width]
            out_ref[0, at, width : 2 * width] = jnp.where(
                lane < width // 2, sums[:, width : 2 * width], top
            )


def attend(first_len, plan, q, kv, sums, new, halves, role="", more=()):
    both, rows, width = q.shape
    slots = kv[0].shape[0] // 2
    part = lambda *tail: pl.BlockSpec((1,) + tail, lambda i, s: (lax.rem(s[0] + i, both), 0, 0))
    whole = lambda a: pl.BlockSpec(a.shape, lambda i, s: (0,) * len(a.shape))
    in_specs = [part(rows, width)] + [whole(a) for a in kv]
    if sums is None:
        in_specs += [whole(a) for a in new[:3]] + [part(*new[3].shape[1:])]
        extra = tuple(new)
    else:
        in_specs.append(whole(sums) if sums.shape[0] == 1 else part(rows, 2 * width))
        extra = (sums,)
    in_specs += [whole(a) for a in more]
    if role == "message":
        out_shape = jax.ShapeDtypeStruct((rows, 2 * width), jnp.bfloat16)
        out_spec = whole(out_shape)
    elif role == "finish":
        tokens = more[1].shape[0]
        out_shape = jax.ShapeDtypeStruct((tokens, rows // tokens * width), jnp.bfloat16)
        out_spec = whole(out_shape)
    else:
        out_shape = jax.ShapeDtypeStruct((halves, rows, 2 * width), jnp.float32)
        out_spec = whole(out_shape) if halves == 1 else part(rows, 2 * width)
    wide = pltpu.VMEM((len(kv) * slots, 2 * width), jnp.bfloat16)
    keys = len(kv) * slots
    return pl.pallas_call(
        functools.partial(attend_kernel, first_len, len(kv), sums is None, role),
        grid_spec=pltpu.PrefetchScalarGridSpec(
            num_scalar_prefetch=1,
            grid=(halves,),
            in_specs=in_specs,
            out_specs=out_spec,
            scratch_shapes=[wide, wide],
        ),
        out_shape=out_shape,
        compiler_params=pltpu.CompilerParams(vmem_limit_bytes=40 * 1024 * 1024),
        cost_estimate=pl.CostEstimate(
            flops=16 * halves * rows * width * keys,
            bytes_accessed=halves * rows * width * 16,
            transcendentals=halves * rows * keys,
        ),
    )(plan, q, *kv, *extra, *more)


def rotate(values, cosine, sine):
    half = values.shape[-1] // 2
    first, second = values[..., :half], values[..., half:]
    return jnp.concatenate(
        [first * cosine - second * sine, second * cosine + first * sine], -1
    ).astype(jnp.bfloat16)


def body(
    queries,
    unrotated_key_rows,
    incoming_value_rows,
    cache_keys,
    stored_value_rows,
    cache_len,
    new_count,
    slot_index,
    out_weight,
):
    ny, nz, nheads = lax.axis_size("y"), lax.axis_size("z"), lax.axis_size("head")
    y, z, core = lax.axis_index("y"), lax.axis_index("z"), lax.axis_index("core")
    convs, slots = slot_index.shape[1], slot_index.shape[2]
    shards = slot_index.shape[0]
    heads, width = queries.shape[1], queries.shape[2]
    here = y * nz + z
    other_core = [(0, 1), (1, 0)]

    def unroll(values, axis, by):
        size = values.shape[axis]
        twice = jnp.concatenate([values, values], axis)
        return lax.dynamic_slice_in_dim(twice, (size - by) % size, size, axis)

    small = jnp.concatenate(
        [
            queries.reshape(convs, slots * heads, width),
            unrotated_key_rows.reshape(convs, slots, width),
            incoming_value_rows.reshape(convs, slots, width),
            jnp.broadcast_to(
                cache_len[0].astype(jnp.bfloat16)[:, None, None], (convs, 16 - 2 * slots, width)
            ),
        ],
        1,
    )
    targets = ((0, 0),) + tuple(leg for group in LEGS for leg in group)
    at = jnp.stack([y, z]).astype(jnp.int32)
    dealt = dict(zip(targets, deal(at, cache_keys, stored_value_rows, (ny, nz), targets)))

    def sent(dy, dz):
        route = [
            (a * nz + b, (a + dy) % ny * nz + (b + dz) % nz) for a in range(ny) for b in range(nz)
        ]
        return lax.ppermute(dealt[dy, dz], ("y", "z"), route)

    depth = out_weight.shape[0] // 2
    other_y = [(0, 1), (1, 0)]
    weight_y = [lax.ppermute(out_weight[:depth], "y", other_y)]
    arrived = [[sent(*leg) for leg in LEGS[0]]]
    joined = lax.optimization_barrier((small, *arrived[0]))
    small, arrived[0] = joined[0], list(joined[1:])
    mine = lax.all_to_all(small, ("y", "z"), 0, 0, tiled=True)
    joined = lax.optimization_barrier((mine, weight_y[0], *arrived[0]))
    mine, weight_y[0], arrived[0] = joined[0], joined[1], list(joined[2:])
    theirs = lax.ppermute(mine, "core", other_core)
    late_legs = [leg for group in LEGS[1:] for leg in group]
    held_back = lax.optimization_barrier(
        tuple(dealt[leg] for leg in late_legs) + (weight_y[0],)
    )
    weight_y[0] = held_back[-1]
    dealt.update(zip(late_legs, held_back))
    arrived += [[sent(*leg) for leg in group] for group in LEGS[1:]]
    rest, _ = lax.optimization_barrier((out_weight[depth:], arrived[-1][-1]))
    weight_y.append(lax.ppermute(rest, "y", other_y))
    core_part, _ = lax.optimization_barrier((out_weight, arrived[0][0]))
    weight_core = lax.ppermute(core_part, "core", other_core)

    both = jnp.where(core == 0, jnp.stack([mine, theirs], 1), jnp.stack([theirs, mine], 1))
    both = both.reshape(shards, small.shape[1], width)
    base = jnp.sum(both[:, slots * heads + 2 * slots, 0].astype(jnp.float32))
    own_lens = mine[:, slots * heads + 2 * slots, 0].astype(jnp.int32)
    senders = [(y - dy) % ny * nz + (z - dz) % nz for dy, dz in targets]
    own_lens = jnp.sum(
        jnp.where(jnp.stack(senders)[:, None] == jnp.arange(convs), own_lens[None, :], 0), 1
    )
    index = lax.dynamic_index_in_dim(slot_index, here, 1, keepdims=False)
    index = index.reshape(shards, 2, slots // 2).transpose(1, 0, 2)
    live = index < new_count[here]
    inverse = 1.0 / 500000.0 ** (jnp.arange(0, width, 2, dtype=jnp.float32) / width)
    angles = (base + index.astype(jnp.float32))[..., None] * inverse
    cosine, sine = jnp.cos(angles), jnp.sin(angles)
    q = both[:, : slots * heads].reshape(shards, 2, slots // 2, heads, width)
    q = q.transpose(1, 3, 0, 2, 4).astype(jnp.float32)
    q = rotate(q, cosine[:, None], sine[:, None])
    tokens = shards * slots // 2
    q = q.reshape(2, heads * tokens, width)

    def new_rows(start):
        rows = both[:, start : start + slots].reshape(shards, 2, slots // 2, width)
        return rows.transpose(1, 0, 2, 3)

    new_k = rotate(new_rows(slots * heads).astype(jnp.float32), cosine, sine)
    new_k = new_k.reshape(2 * tokens, width)
    new_v = new_rows(slots * heads + slots).reshape(2 * tokens, width)
    kept = live & (jnp.arange(shards)[None, :, None] % 2 == core)
    key_index = jnp.where(kept, index.astype(jnp.float32), CLOSED).reshape(1, 2 * tokens)
    key_index = jnp.broadcast_to(key_index, (8, 2 * tokens))
    row_index = jnp.broadcast_to(
        index.astype(jnp.float32).reshape(2, 1, tokens, 1), (2, STEP // tokens, tokens, 128)
    ).reshape(2, STEP, 128)

    def plan(which):
        return jnp.concatenate([jnp.full((1,), which, jnp.int32), own_lens])

    joined = lax.optimization_barrier((q, *arrived[1]))
    q, arrived[1] = joined[0], list(joined[1:])
    start = plan(0)
    sums = attend(1, start, q, [dealt[0, 0]], None, (new_k, new_v, key_index, row_index), 2)
    at_len = 2
    for blocks in arrived[:-2]:
        sums = attend(at_len, start, q, blocks, sums, None, 2)
        at_len += len(blocks)
    ours, others = plan(core), plan(1 - core)
    last_len = at_len + len(arrived[-2])
    message = attend(at_len, others, q, arrived[-2], sums, None, 1)
    message = attend(last_len, others, q, arrived[-1], message, None, 1, "message")
    message = lax.ppermute(message, "core", other_core)
    live_rows = lax.dynamic_index_in_dim(live, core, 0, keepdims=False)
    live_rows = jnp.broadcast_to(live_rows.astype(jnp.float32).reshape(tokens, 1), (tokens, 128))
    sums = attend(at_len, ours, q, arrived[-2], sums, None, 1)
    attended = attend(
        last_len, ours, q, arrived[-1], sums, None, 1, "finish", (message, live_rows)
    )

    attended = attended.reshape(nheads, tokens // nheads, heads * width)
    up = [(i, (i + 1) % nz) for i in range(nz)]
    down = [(i, (i - 1) % nz) for i in range(nz)]
    held = {0: attended}
    for step in range(1, nz // 2):
        held[-step % nz] = lax.ppermute(held[(1 - step) % nz], "z", up)
        held[step] = lax.ppermute(held[step - 1], "z", down)
    first_half, _ = lax.optimization_barrier((weight_y[0], attended))
    second_half, _ = lax.optimization_barrier((weight_y[1], held[2]))
    weight_far = jnp.concatenate([first_half, second_half], 0)
    weight_both = jnp.concatenate(
        [
            lax.ppermute(first_half, "core", other_core),
            lax.ppermute(second_half, "core", other_core),
        ],
        0,
    )
    near = [
        jnp.where(core == 0, out_weight, weight_core),
        jnp.where(core == 0, weight_core, out_weight),
    ]
    far = [
        jnp.where(core == 0, weight_far, weight_both),
        jnp.where(core == 0, weight_both, weight_far),
    ]
    weights = jnp.stack(
        [jnp.where(y == 0, a, b) for a, b in zip(near, far)]
        + [jnp.where(y == 0, b, a) for a, b in zip(near, far)]
    )

    def parts_of(which):
        rows = jnp.stack([held[k] for k in which], 1)
        rows = rows.reshape(-1, heads * width)
        parts = jnp.einsum("rk,wkn->wrn", rows, weights, preferred_element_type=jnp.float32)
        return parts.astype(jnp.bfloat16).reshape(4 * nheads, -1, out_weight.shape[1])

    early = (0, 1, 2, nz - 2, nz - 1)
    late = tuple(range(3, nz - 2))
    early_parts = parts_of(early)
    middle = nz // 2
    from_below, from_above, early_parts = lax.optimization_barrier(
        (held[middle + 1], held[middle - 1], early_parts)
    )
    cut = max(nheads // 2, 1)
    held[middle] = jnp.concatenate(
        [
            lax.ppermute(from_below[:cut], "z", up),
            lax.ppermute(from_above[cut:], "z", down),
        ],
        0,
    )
    parts = jnp.concatenate([early_parts, parts_of(late)], 1)
    got = lax.all_to_all(parts, ("y", "core", "head"), 0, 0, tiled=True)
    got = got.reshape(ny, 2, nheads, nz, tokens // nheads, -1)
    done = jnp.sum(got.astype(jnp.float32), 2).astype(jnp.bfloat16)
    order = early + late
    done = unroll(jnp.stack([done[:, :, order.index(k)] for k in range(nz)], 0), 0, z)
    done = done.reshape(nz, ny, 2, shards // nheads, slots // 2, -1)
    done = done.transpose(3, 1, 0, 2, 4, 5)
    return done.reshape(shards // nheads * convs * slots, -1)


def solution(mesh):
    blk, head = mesh.shape["blk"], mesh.shape["head"]
    fine = Mesh(mesh.devices.reshape(2, blk // 4, 2, head), ("y", "z", "core", "head"))
    blk = ("y", "z", "core")
    return jax.shard_map(
        body,
        mesh=fine,
        in_specs=(
            P(blk, "head", None),
            P(blk, "head", None),
            P(blk, "head", None),
            P(blk, None, "head", None, None),
            P(blk, None, "head", None, None),
            P(blk, None),
            P(),
            P(),
            P("head", blk),
        ),
        out_specs=P("head", blk),
        check_vma=False,
    )
```

```python
import functools

import jax
import jax.numpy as jnp
from jax import lax
from jax.experimental import pallas as pl
from jax.experimental.pallas import tpu as pltpu
from jax.sharding import Mesh, PartitionSpec as P

LOG2_E = 1.4426950408889634
CLOSED = 1.0e9
SHUT = -1.0e30
STEP = 256
LEGS = (
    ((0, 1), (0, 4), (0, 3), (0, -3)),
    ((0, 2), (0, -2), (0, -1)),
    ((1, 4), (1, 3), (1, -3), (1, 2)),
    ((1, -2), (1, 1), (1, -1), (1, 0)),
)


def deal_kernel(targets, at_ref, keys_ref, values_ref, *refs):
    outs, (stage, in_sems, out_sems) = refs[:-3], refs[-3:]
    ny, nz = targets[0]
    slots = keys_ref.shape[3]
    copies = []
    for i, (dy, dz) in enumerate(targets[1]):
        conversation = lax.rem(at_ref[0] + dy, ny) * nz + lax.rem(at_ref[1] + (dz + nz) % nz, nz)
        for j, ref in enumerate((keys_ref, values_ref)):
            copy = pltpu.make_async_copy(
                ref.at[0, conversation, 0], stage.at[i, pl.ds(j * slots, slots)], in_sems.at[i, j]
            )
            copy.start()
            copies.append(copy)
    leaving = []
    for i in range(len(outs)):
        copies[2 * i].wait()
        copies[2 * i + 1].wait()
        copy = pltpu.make_async_copy(stage.at[i], outs[i], out_sems.at[i])
        copy.start()
        leaving.append(copy)
    for copy in leaving:
        copy.wait()


def deal(at, keys, values, grid, targets):
    slots, width = keys.shape[3], keys.shape[4]
    anywhere = pl.BlockSpec(memory_space=pl.ANY)
    count = len(targets)
    return pl.pallas_call(
        functools.partial(deal_kernel, (grid, targets)),
        in_specs=[pl.BlockSpec(memory_space=pltpu.SMEM), anywhere, anywhere],
        out_specs=[anywhere] * count,
        out_shape=[jax.ShapeDtypeStruct((2 * slots, width), jnp.bfloat16)] * count,
        scratch_shapes=[
            pltpu.VMEM((count, 2 * slots, width), jnp.bfloat16),
            pltpu.SemaphoreType.DMA((count, 2)),
            pltpu.SemaphoreType.DMA((count,)),
        ],
    )(at, keys, values)


def attend_kernel(first_len, shards, first, role, plan_ref, q_ref, *refs):
    refs = list(refs)
    keys_ref, values_ref = refs[-2:]
    kv_refs = [refs.pop(0) for _ in range(shards)]
    if first:
        new_k_ref, new_v_ref, key_index_ref, row_index_ref = [refs.pop(0) for _ in range(4)]
    else:
        sums_ref = refs.pop(0)
    if role == "finish":
        message_ref, live_ref = refs.pop(0), refs.pop(0)
    out_ref = refs.pop(0)
    rows, width = q_ref.shape[1], q_ref.shape[2]
    slots = kv_refs[0].shape[0] // 2
    scale = LOG2_E / width**0.5

    @pl.when(pl.program_id(0) == 0)
    def _():
        first_lane = lax.broadcasted_iota(jnp.int32, (slots, width), 1) == 0
        slot = lax.broadcasted_iota(jnp.int32, (slots, width), 0)
        for i, ref in enumerate(kv_refs):
            at = slice(i * slots, (i + 1) * slots)
            keys_ref[at, 0:width] = ref[0:slots, :]
            shut = first_lane & (slot >= plan_ref[first_len + i])
            keys_ref[at, width : 2 * width] = jnp.where(shut, SHUT, 0.0).astype(jnp.bfloat16)
            values_ref[at, 0:width] = ref[slots : 2 * slots, :]
            values_ref[at, width : 2 * width] = jnp.ones((slots, width), jnp.bfloat16)

    lane = lax.broadcasted_iota(jnp.int32, (STEP, width), 1)
    unit = jnp.where(lane == 0, 1.0, 0.0).astype(jnp.bfloat16)
    if first:
        seen = key_index_ref[0:1, :] <= row_index_ref[0]
        ones = jnp.ones((new_v_ref.shape[0], width), jnp.bfloat16)

    if role == "finish":
        row = lax.broadcasted_iota(jnp.int32, (width, 2 * width), 0)
        group = jnp.where(lax.broadcasted_iota(jnp.int32, (width, 2 * width), 1) < width, 0, 3)
        spread = jnp.where((row >= group) & (row < group + 3), 1.0, 0.0).astype(jnp.bfloat16)

    def score(a, b):
        return lax.dot_general(a, b, (((1,), (1,)), ((), ())), preferred_element_type=jnp.float32)

    def scores(step):
        q = q_ref[0, step * STEP : (step + 1) * STEP, :]
        wide = jnp.concatenate([q, unit], 1)
        found = [score(wide, keys_ref[i * slots : (i + 1) * slots, :]) for i in range(shards)]
        if first:
            found.append(jnp.where(seen, score(q, new_k_ref[...]), SHUT))
        return found

    def highest(found, step):
        top = jnp.max(functools.reduce(jnp.maximum, found[:shards]), axis=1, keepdims=True)
        if first:
            return jnp.maximum(top, jnp.max(found[shards], axis=1, keepdims=True))
        before = sums_ref[0, step * STEP : (step + 1) * STEP, 2 * width - 1 : 2 * width]
        return jnp.maximum(top, before)

    steps = rows // STEP
    after = scores(0)
    after_top = highest(after, 0)
    for step in range(steps):
        at = slice(step * STEP, (step + 1) * STEP)
        found, top = after, after_top
        if step + 1 < steps:
            after = scores(step + 1)
        low = top * scale
        if first:
            sums = jnp.zeros((STEP, 2 * width), jnp.float32)
        else:
            sums = sums_ref[0, at, :]
            sums = sums * jnp.exp2(sums[:, 2 * width - 1 : 2 * width] * scale - low)
        for i, s in enumerate(found):
            w = jnp.exp2(s * scale - low).astype(jnp.bfloat16)
            if i < shards:
                v = values_ref[i * slots : (i + 1) * slots, :]
            else:
                v = jnp.concatenate([new_v_ref[...], ones], 1)
            sums = sums + jnp.dot(w, v, preferred_element_type=jnp.float32)
        if step + 1 < steps:
            after_top = highest(after, step + 1)
        if role == "message":
            tail = jnp.zeros((STEP, width), jnp.float32)
            total = sums[:, width : 2 * width]
            for i, value in enumerate((total, jnp.broadcast_to(top, total.shape))):
                for j in range(3):
                    part = value.astype(jnp.bfloat16).astype(jnp.float32)
                    tail = jnp.where(lane == 3 * i + j, part, tail)
                    value = value - part
            out_ref[at, 0:width] = sums[:, 0:width].astype(jnp.bfloat16)
            out_ref[at, width : 2 * width] = tail.astype(jnp.bfloat16)
        elif role == "finish":
            stats = jnp.dot(
                message_ref[at, width : 2 * width], spread, preferred_element_type=jnp.float32
            )
            highest_of_all = jnp.maximum(top, stats[:, width:])
            a = jnp.exp2((top - highest_of_all) * scale)
            b = jnp.exp2((stats[:, width:] - highest_of_all) * scale)
            total = sums[:, width : width + 1] * a + stats[:, :width] * b
            other = message_ref[at, 0:width].astype(jnp.float32)
            mixed = (sums[:, 0:width] * a + other * b) / total
            tokens = live_ref.shape[0]
            for i in range(STEP // tokens):
                head = step * (STEP // tokens) + i
                block = mixed[i * tokens : (i + 1) * tokens, :] * live_ref[...]
                out_ref[:, head * width : (head + 1) * width] = block.astype(jnp.bfloat16)
        else:
            out_ref[0, at, 0:width] = sums[:, 0:width]
            out_ref[0, at, width : 2 * width] = jnp.where(
                lane < width // 2, sums[:, width : 2 * width], top
            )


def attend(first_len, plan, q, kv, sums, new, halves, role="", more=()):
    both, rows, width = q.shape
    slots = kv[0].shape[0] // 2
    part = lambda *tail: pl.BlockSpec((1,) + tail, lambda i, s: (lax.rem(s[0] + i, both), 0, 0))
    whole = lambda a: pl.BlockSpec(a.shape, lambda i, s: (0,) * len(a.shape))
    in_specs = [part(rows, width)] + [whole(a) for a in kv]
    if sums is None:
        in_specs += [whole(a) for a in new[:3]] + [part(*new[3].shape[1:])]
        extra = tuple(new)
    else:
        in_specs.append(whole(sums) if sums.shape[0] == 1 else part(rows, 2 * width))
        extra = (sums,)
    in_specs += [whole(a) for a in more]
    if role == "message":
        out_shape = jax.ShapeDtypeStruct((rows, 2 * width), jnp.bfloat16)
        out_spec = whole(out_shape)
    elif role == "finish":
        tokens = more[1].shape[0]
        out_shape = jax.ShapeDtypeStruct((tokens, rows // tokens * width), jnp.bfloat16)
        out_spec = whole(out_shape)
    else:
        out_shape = jax.ShapeDtypeStruct((halves, rows, 2 * width), jnp.float32)
        out_spec = whole(out_shape) if halves == 1 else part(rows, 2 * width)
    wide = pltpu.VMEM((len(kv) * slots, 2 * width), jnp.bfloat16)
    keys = len(kv) * slots
    return pl.pallas_call(
        functools.partial(attend_kernel, first_len, len(kv), sums is None, role),
        grid_spec=pltpu.PrefetchScalarGridSpec(
            num_scalar_prefetch=1,
            grid=(halves,),
            in_specs=in_specs,
            out_specs=out_spec,
            scratch_shapes=[wide, wide],
        ),
        out_shape=out_shape,
        compiler_params=pltpu.CompilerParams(vmem_limit_bytes=40 * 1024 * 1024),
        cost_estimate=pl.CostEstimate(
            flops=16 * halves * rows * width * keys,
            bytes_accessed=halves * rows * width * 16,
            transcendentals=halves * rows * keys,
        ),
    )(plan, q, *kv, *extra, *more)


def rotate(values, cosine, sine):
    half = values.shape[-1] // 2
    first, second = values[..., :half], values[..., half:]
    return jnp.concatenate(
        [first * cosine - second * sine, second * cosine + first * sine], -1
    ).astype(jnp.bfloat16)


def body(
    queries,
    unrotated_key_rows,
    incoming_value_rows,
    cache_keys,
    stored_value_rows,
    cache_len,
    new_count,
    slot_index,
    out_weight,
):
    ny, nz, nheads = lax.axis_size("y"), lax.axis_size("z"), lax.axis_size("head")
    y, z, core = lax.axis_index("y"), lax.axis_index("z"), lax.axis_index("core")
    convs, slots = slot_index.shape[1], slot_index.shape[2]
    shards = slot_index.shape[0]
    heads, width = queries.shape[1], queries.shape[2]
    here = y * nz + z
    other_core = [(0, 1), (1, 0)]

    def unroll(values, axis, by):
        size = values.shape[axis]
        twice = jnp.concatenate([values, values], axis)
        return lax.dynamic_slice_in_dim(twice, (size - by) % size, size, axis)

    small = jnp.concatenate(
        [
            queries.reshape(convs, slots * heads, width),
            unrotated_key_rows.reshape(convs, slots, width),
            incoming_value_rows.reshape(convs, slots, width),
            jnp.broadcast_to(
                cache_len[0].astype(jnp.bfloat16)[:, None, None], (convs, 16 - 2 * slots, width)
            ),
        ],
        1,
    )
    targets = ((0, 0),) + tuple(leg for group in LEGS for leg in group)
    at = jnp.stack([y, z]).astype(jnp.int32)
    dealt = dict(zip(targets, deal(at, cache_keys, stored_value_rows, (ny, nz), targets)))

    def sent(dy, dz):
        route = [
            (a * nz + b, (a + dy) % ny * nz + (b + dz) % nz) for a in range(ny) for b in range(nz)
        ]
        return lax.ppermute(dealt[dy, dz], ("y", "z"), route)

    depth = out_weight.shape[0] * 5 // 8
    other_y = [(0, 1), (1, 0)]
    weight_y = [lax.ppermute(out_weight[:depth], "y", other_y)]
    arrived = [[sent(*leg) for leg in LEGS[0]]]
    joined = lax.optimization_barrier((small, weight_y[0], *arrived[0]))
    small, weight_y[0], arrived[0] = joined[0], joined[1], list(joined[2:])
    late_legs = [leg for group in LEGS[1:] for leg in group]
    held_back = lax.optimization_barrier(
        tuple(dealt[leg] for leg in late_legs) + (weight_y[0],)
    )
    weight_y[0] = held_back[-1]
    dealt.update(zip(late_legs, held_back))
    arrived += [[sent(*leg) for leg in group] for group in LEGS[1:]]
    mine = lax.all_to_all(small, ("y", "z"), 0, 0, tiled=True)
    joined = lax.optimization_barrier((mine, *arrived[1]))
    mine, arrived[1] = joined[0], list(joined[1:])
    theirs = lax.ppermute(mine, "core", other_core)
    rest, _ = lax.optimization_barrier((out_weight, arrived[-1][-1]))
    weight_y.append(lax.ppermute(rest[depth:], "y", other_y))
    core_part, _ = lax.optimization_barrier((out_weight, arrived[0][0]))
    weight_core = lax.ppermute(core_part, "core", other_core)

    both = jnp.where(core == 0, jnp.stack([mine, theirs], 1), jnp.stack([theirs, mine], 1))
    both = both.reshape(shards, small.shape[1], width)
    base = jnp.sum(both[:, slots * heads + 2 * slots, 0].astype(jnp.float32))
    own_lens = mine[:, slots * heads + 2 * slots, 0].astype(jnp.int32)
    senders = [(y - dy) % ny * nz + (z - dz) % nz for dy, dz in targets]
    own_lens = jnp.sum(
        jnp.where(jnp.stack(senders)[:, None] == jnp.arange(convs), own_lens[None, :], 0), 1
    )
    index = lax.dynamic_index_in_dim(slot_index, here, 1, keepdims=False)
    index = index.reshape(shards, 2, slots // 2).transpose(1, 0, 2)
    live = index < new_count[here]
    inverse = 1.0 / 500000.0 ** (jnp.arange(0, width, 2, dtype=jnp.float32) / width)
    angles = (base + index.astype(jnp.float32))[..., None] * inverse
    cosine, sine = jnp.cos(angles), jnp.sin(angles)
    q = both[:, : slots * heads].reshape(shards, 2, slots // 2, heads, width)
    q = q.transpose(1, 3, 0, 2, 4).astype(jnp.float32)
    q = rotate(q, cosine[:, None], sine[:, None])
    tokens = shards * slots // 2
    q = q.reshape(2, heads * tokens, width)

    def new_rows(start):
        rows = both[:, start : start + slots].reshape(shards, 2, slots // 2, width)
        return rows.transpose(1, 0, 2, 3)

    new_k = rotate(new_rows(slots * heads).astype(jnp.float32), cosine, sine)
    new_k = new_k.reshape(2 * tokens, width)
    new_v = new_rows(slots * heads + slots).reshape(2 * tokens, width)
    kept = live & (jnp.arange(shards)[None, :, None] % 2 == core)
    key_index = jnp.where(kept, index.astype(jnp.float32), CLOSED).reshape(1, 2 * tokens)
    key_index = jnp.broadcast_to(key_index, (8, 2 * tokens))
    row_index = jnp.broadcast_to(
        index.astype(jnp.float32).reshape(2, 1, tokens, 1), (2, STEP // tokens, tokens, 128)
    ).reshape(2, STEP, 128)

    def plan(which):
        return jnp.concatenate([jnp.full((1,), which, jnp.int32), own_lens])

    start = plan(0)
    sums = attend(1, start, q, [dealt[0, 0]], None, (new_k, new_v, key_index, row_index), 2)
    at_len = 2
    for blocks in arrived[:-2]:
        sums = attend(at_len, start, q, blocks, sums, None, 2)
        at_len += len(blocks)
    ours, others = plan(core), plan(1 - core)
    last_len = at_len + len(arrived[-2])
    message = attend(at_len, others, q, arrived[-2], sums, None, 1)
    message = attend(last_len, others, q, arrived[-1], message, None, 1, "message")
    message = lax.ppermute(message, "core", other_core)
    live_rows = lax.dynamic_index_in_dim(live, core, 0, keepdims=False)
    live_rows = jnp.broadcast_to(live_rows.astype(jnp.float32).reshape(tokens, 1), (tokens, 128))
    sums = attend(at_len, ours, q, arrived[-2], sums, None, 1)
    attended = attend(
        last_len, ours, q, arrived[-1], sums, None, 1, "finish", (message, live_rows)
    )

    attended = attended.reshape(nheads, tokens // nheads, heads * width)
    up = [(i, (i + 1) % nz) for i in range(nz)]
    down = [(i, (i - 1) % nz) for i in range(nz)]
    held = {0: attended}
    for step in range(1, nz // 2):
        held[-step % nz] = lax.ppermute(held[(1 - step) % nz], "z", up)
        held[step] = lax.ppermute(held[step - 1], "z", down)
    first_half, _ = lax.optimization_barrier((weight_y[0], attended))
    second_half, _ = lax.optimization_barrier((weight_y[1], held[2]))
    weight_far = jnp.concatenate([first_half, second_half], 0)
    weight_both = jnp.concatenate(
        [
            lax.ppermute(first_half, "core", other_core),
            lax.ppermute(second_half, "core", other_core),
        ],
        0,
    )
    near = [
        jnp.where(core == 0, out_weight, weight_core),
        jnp.where(core == 0, weight_core, out_weight),
    ]
    far = [
        jnp.where(core == 0, weight_far, weight_both),
        jnp.where(core == 0, weight_both, weight_far),
    ]
    weights = jnp.stack(
        [jnp.where(y == 0, a, b) for a, b in zip(near, far)]
        + [jnp.where(y == 0, b, a) for a, b in zip(near, far)]
    )

    def parts_of(which):
        rows = jnp.stack([held[k] for k in which], 1)
        rows = rows.reshape(-1, heads * width)
        parts = jnp.einsum("rk,wkn->wrn", rows, weights, preferred_element_type=jnp.float32)
        return parts.astype(jnp.bfloat16).reshape(4 * nheads, -1, out_weight.shape[1])

    early = (0, 1, 2, nz - 2, nz - 1)
    late = tuple(range(3, nz - 2))
    early_parts = parts_of(early)
    middle = nz // 2
    from_below, from_above, early_parts = lax.optimization_barrier(
        (held[middle + 1], held[middle - 1], early_parts)
    )
    cut = max(nheads // 2, 1)
    held[middle] = jnp.concatenate(
        [
            lax.ppermute(from_below[:cut], "z", up),
            lax.ppermute(from_above[cut:], "z", down),
        ],
        0,
    )
    parts = jnp.concatenate([early_parts, parts_of(late)], 1)
    got = lax.all_to_all(parts, ("y", "core", "head"), 0, 0, tiled=True)
    got = got.reshape(ny, 2, nheads, nz, tokens // nheads, -1)
    done = jnp.sum(got.astype(jnp.float32), 2).astype(jnp.bfloat16)
    order = early + late
    done = unroll(jnp.stack([done[:, :, order.index(k)] for k in range(nz)], 0), 0, z)
    done = done.reshape(nz, ny, 2, shards // nheads, slots // 2, -1)
    done = done.transpose(3, 1, 0, 2, 4, 5)
    return done.reshape(shards // nheads * convs * slots, -1)


def solution(mesh):
    blk, head = mesh.shape["blk"], mesh.shape["head"]
    fine = Mesh(mesh.devices.reshape(2, blk // 4, 2, head), ("y", "z", "core", "head"))
    blk = ("y", "z", "core")
    return jax.shard_map(
        body,
        mesh=fine,
        in_specs=(
            P(blk, "head", None),
            P(blk, "head", None),
            P(blk, "head", None),
            P(blk, None, "head", None, None),
            P(blk, None, "head", None, None),
            P(blk, None),
            P(),
            P(),
            P("head", blk),
        ),
        out_specs=P("head", blk),
        check_vma=False,
    )
```

```python
import functools

import jax
import jax.numpy as jnp
from jax import lax
from jax.experimental import pallas as pl
from jax.experimental.pallas import tpu as pltpu
from jax.sharding import Mesh, PartitionSpec as P

LOG2_E = 1.4426950408889634
CLOSED = 1.0e9
SHUT = -1.0e30
STEP = 256
LEGS = (
    ((0, 4), (0, 3), (0, -3)),
    ((0, 2), (0, -2), (0, 1), (0, -1)),
    ((1, 4), (1, 3), (1, -3), (1, 2)),
    ((1, -2), (1, 1), (1, -1), (1, 0)),
)


def deal_kernel(targets, at_ref, keys_ref, values_ref, *refs):
    outs, (stage, in_sems, out_sems) = refs[:-3], refs[-3:]
    ny, nz = targets[0]
    slots = keys_ref.shape[3]
    copies = []
    for i, (dy, dz) in enumerate(targets[1]):
        conversation = lax.rem(at_ref[0] + dy, ny) * nz + lax.rem(at_ref[1] + (dz + nz) % nz, nz)
        for j, ref in enumerate((keys_ref, values_ref)):
            copy = pltpu.make_async_copy(
                ref.at[0, conversation, 0], stage.at[i, pl.ds(j * slots, slots)], in_sems.at[i, j]
            )
            copy.start()
            copies.append(copy)
    leaving = []
    for i in range(len(outs)):
        copies[2 * i].wait()
        copies[2 * i + 1].wait()
        copy = pltpu.make_async_copy(stage.at[i], outs[i], out_sems.at[i])
        copy.start()
        leaving.append(copy)
    for copy in leaving:
        copy.wait()


def deal(at, keys, values, grid, targets):
    slots, width = keys.shape[3], keys.shape[4]
    anywhere = pl.BlockSpec(memory_space=pl.ANY)
    count = len(targets)
    return pl.pallas_call(
        functools.partial(deal_kernel, (grid, targets)),
        in_specs=[pl.BlockSpec(memory_space=pltpu.SMEM), anywhere, anywhere],
        out_specs=[anywhere] * count,
        out_shape=[jax.ShapeDtypeStruct((2 * slots, width), jnp.bfloat16)] * count,
        scratch_shapes=[
            pltpu.VMEM((count, 2 * slots, width), jnp.bfloat16),
            pltpu.SemaphoreType.DMA((count, 2)),
            pltpu.SemaphoreType.DMA((count,)),
        ],
    )(at, keys, values)


def attend_kernel(first_len, shards, first, role, plan_ref, q_ref, *refs):
    refs = list(refs)
    keys_ref, values_ref = refs[-2:]
    kv_refs = [refs.pop(0) for _ in range(shards)]
    if first:
        new_k_ref, new_v_ref, key_index_ref, row_index_ref = [refs.pop(0) for _ in range(4)]
    else:
        sums_ref = refs.pop(0)
    if role == "finish":
        message_ref, live_ref = refs.pop(0), refs.pop(0)
    out_ref = refs.pop(0)
    rows, width = q_ref.shape[1], q_ref.shape[2]
    slots = kv_refs[0].shape[0] // 2
    scale = LOG2_E / width**0.5

    @pl.when(pl.program_id(0) == 0)
    def _():
        first_lane = lax.broadcasted_iota(jnp.int32, (slots, width), 1) == 0
        slot = lax.broadcasted_iota(jnp.int32, (slots, width), 0)
        for i, ref in enumerate(kv_refs):
            at = slice(i * slots, (i + 1) * slots)
            keys_ref[at, 0:width] = ref[0:slots, :]
            shut = first_lane & (slot >= plan_ref[first_len + i])
            keys_ref[at, width : 2 * width] = jnp.where(shut, SHUT, 0.0).astype(jnp.bfloat16)
            values_ref[at, 0:width] = ref[slots : 2 * slots, :]
            values_ref[at, width : 2 * width] = jnp.ones((slots, width), jnp.bfloat16)

    lane = lax.broadcasted_iota(jnp.int32, (STEP, width), 1)
    unit = jnp.where(lane == 0, 1.0, 0.0).astype(jnp.bfloat16)
    if first:
        seen = key_index_ref[0:1, :] <= row_index_ref[0]
        ones = jnp.ones((new_v_ref.shape[0], width), jnp.bfloat16)

    if role == "finish":
        row = lax.broadcasted_iota(jnp.int32, (width, 2 * width), 0)
        group = jnp.where(lax.broadcasted_iota(jnp.int32, (width, 2 * width), 1) < width, 0, 3)
        spread = jnp.where((row >= group) & (row < group + 3), 1.0, 0.0).astype(jnp.bfloat16)

    def score(a, b):
        return lax.dot_general(a, b, (((1,), (1,)), ((), ())), preferred_element_type=jnp.float32)

    def scores(step):
        q = q_ref[0, step * STEP : (step + 1) * STEP, :]
        wide = jnp.concatenate([q, unit], 1)
        found = [score(wide, keys_ref[i * slots : (i + 1) * slots, :]) for i in range(shards)]
        if first:
            found.append(jnp.where(seen, score(q, new_k_ref[...]), SHUT))
        return found

    def highest(found, step):
        top = jnp.max(functools.reduce(jnp.maximum, found[:shards]), axis=1, keepdims=True)
        if first:
            return jnp.maximum(top, jnp.max(found[shards], axis=1, keepdims=True))
        before = sums_ref[0, step * STEP : (step + 1) * STEP, 2 * width - 1 : 2 * width]
        return jnp.maximum(top, before)

    steps = rows // STEP
    after = scores(0)
    after_top = highest(after, 0)
    for step in range(steps):
        at = slice(step * STEP, (step + 1) * STEP)
        found, top = after, after_top
        if step + 1 < steps:
            after = scores(step + 1)
        low = top * scale
        if first:
            sums = jnp.zeros((STEP, 2 * width), jnp.float32)
        else:
            sums = sums_ref[0, at, :]
            sums = sums * jnp.exp2(sums[:, 2 * width - 1 : 2 * width] * scale - low)
        for i, s in enumerate(found):
            w = jnp.exp2(s * scale - low).astype(jnp.bfloat16)
            if i < shards:
                v = values_ref[i * slots : (i + 1) * slots, :]
            else:
                v = jnp.concatenate([new_v_ref[...], ones], 1)
            sums = sums + jnp.dot(w, v, preferred_element_type=jnp.float32)
        if step + 1 < steps:
            after_top = highest(after, step + 1)
        if role == "message":
            tail = jnp.zeros((STEP, width), jnp.float32)
            total = sums[:, width : 2 * width]
            for i, value in enumerate((total, jnp.broadcast_to(top, total.shape))):
                for j in range(3):
                    part = value.astype(jnp.bfloat16).astype(jnp.float32)
                    tail = jnp.where(lane == 3 * i + j, part, tail)
                    value = value - part
            out_ref[at, 0:width] = sums[:, 0:width].astype(jnp.bfloat16)
            out_ref[at, width : 2 * width] = tail.astype(jnp.bfloat16)
        elif role == "finish":
            stats = jnp.dot(
                message_ref[at, width : 2 * width], spread, preferred_element_type=jnp.float32
            )
            highest_of_all = jnp.maximum(top, stats[:, width:])
            a = jnp.exp2((top - highest_of_all) * scale)
            b = jnp.exp2((stats[:, width:] - highest_of_all) * scale)
            total = sums[:, width : width + 1] * a + stats[:, :width] * b
            other = message_ref[at, 0:width].astype(jnp.float32)
            mixed = (sums[:, 0:width] * a + other * b) / total
            tokens = live_ref.shape[0]
            for i in range(STEP // tokens):
                head = step * (STEP // tokens) + i
                block = mixed[i * tokens : (i + 1) * tokens, :] * live_ref[...]
                out_ref[:, head * width : (head + 1) * width] = block.astype(jnp.bfloat16)
        else:
            out_ref[0, at, 0:width] = sums[:, 0:width]
            out_ref[0, at, width : 2 * width] = jnp.where(
                lane < width // 2, sums[:, width : 2 * width], top
            )


def attend(first_len, plan, q, kv, sums, new, halves, role="", more=()):
    both, rows, width = q.shape
    slots = kv[0].shape[0] // 2
    part = lambda *tail: pl.BlockSpec((1,) + tail, lambda i, s: (lax.rem(s[0] + i, both), 0, 0))
    whole = lambda a: pl.BlockSpec(a.shape, lambda i, s: (0,) * len(a.shape))
    in_specs = [part(rows, width)] + [whole(a) for a in kv]
    if sums is None:
        in_specs += [whole(a) for a in new[:3]] + [part(*new[3].shape[1:])]
        extra = tuple(new)
    else:
        in_specs.append(whole(sums) if sums.shape[0] == 1 else part(rows, 2 * width))
        extra = (sums,)
    in_specs += [whole(a) for a in more]
    if role == "message":
        out_shape = jax.ShapeDtypeStruct((rows, 2 * width), jnp.bfloat16)
        out_spec = whole(out_shape)
    elif role == "finish":
        tokens = more[1].shape[0]
        out_shape = jax.ShapeDtypeStruct((tokens, rows // tokens * width), jnp.bfloat16)
        out_spec = whole(out_shape)
    else:
        out_shape = jax.ShapeDtypeStruct((halves, rows, 2 * width), jnp.float32)
        out_spec = whole(out_shape) if halves == 1 else part(rows, 2 * width)
    wide = pltpu.VMEM((len(kv) * slots, 2 * width), jnp.bfloat16)
    keys = len(kv) * slots
    return pl.pallas_call(
        functools.partial(attend_kernel, first_len, len(kv), sums is None, role),
        grid_spec=pltpu.PrefetchScalarGridSpec(
            num_scalar_prefetch=1,
            grid=(halves,),
            in_specs=in_specs,
            out_specs=out_spec,
            scratch_shapes=[wide, wide],
        ),
        out_shape=out_shape,
        compiler_params=pltpu.CompilerParams(vmem_limit_bytes=40 * 1024 * 1024),
        cost_estimate=pl.CostEstimate(
            flops=16 * halves * rows * width * keys,
            bytes_accessed=halves * rows * width * 16,
            transcendentals=halves * rows * keys,
        ),
    )(plan, q, *kv, *extra, *more)


def rotate(values, cosine, sine):
    half = values.shape[-1] // 2
    first, second = values[..., :half], values[..., half:]
    return jnp.concatenate(
        [first * cosine - second * sine, second * cosine + first * sine], -1
    ).astype(jnp.bfloat16)


def body(
    queries,
    unrotated_key_rows,
    incoming_value_rows,
    cache_keys,
    stored_value_rows,
    cache_len,
    new_count,
    slot_index,
    out_weight,
):
    ny, nz, nheads = lax.axis_size("y"), lax.axis_size("z"), lax.axis_size("head")
    y, z, core = lax.axis_index("y"), lax.axis_index("z"), lax.axis_index("core")
    convs, slots = slot_index.shape[1], slot_index.shape[2]
    shards = slot_index.shape[0]
    heads, width = queries.shape[1], queries.shape[2]
    here = y * nz + z
    other_core = [(0, 1), (1, 0)]

    def unroll(values, axis, by):
        size = values.shape[axis]
        twice = jnp.concatenate([values, values], axis)
        return lax.dynamic_slice_in_dim(twice, (size - by) % size, size, axis)

    small = jnp.concatenate(
        [
            queries.reshape(convs, slots * heads, width),
            unrotated_key_rows.reshape(convs, slots, width),
            incoming_value_rows.reshape(convs, slots, width),
            jnp.broadcast_to(
                cache_len[0].astype(jnp.bfloat16)[:, None, None], (convs, 16 - 2 * slots, width)
            ),
        ],
        1,
    )
    mine = lax.all_to_all(small, ("y", "z"), 0, 0, tiled=True)
    theirs = lax.ppermute(mine, "core", other_core)

    targets = ((0, 0),) + tuple(leg for group in LEGS for leg in group)
    at = jnp.stack([y, z]).astype(jnp.int32)
    dealt = dict(zip(targets, deal(at, cache_keys, stored_value_rows, (ny, nz), targets)))

    def sent(dy, dz):
        route = [
            (a * nz + b, (a + dy) % ny * nz + (b + dz) % nz) for a in range(ny) for b in range(nz)
        ]
        return lax.ppermute(dealt[dy, dz], ("y", "z"), route)

    depth = out_weight.shape[0] // 2
    other_y = [(0, 1), (1, 0)]
    weight_y = [lax.ppermute(out_weight[:depth], "y", other_y)]
    arrived = []
    for i, group in enumerate(LEGS):
        if i == 1:
            late_legs = [leg for some in LEGS[1:] for leg in some]
            held_back = lax.optimization_barrier(
                tuple(dealt[leg] for leg in late_legs) + (weight_y[0],)
            )
            weight_y[0] = held_back[-1]
            dealt.update(zip(late_legs, held_back))
        arrived.append([sent(*leg) for leg in group])
    rest, _ = lax.optimization_barrier((out_weight[depth:], arrived[-1][-1]))
    weight_y.append(lax.ppermute(rest, "y", other_y))
    core_part, _ = lax.optimization_barrier((out_weight, arrived[0][0]))
    weight_core = lax.ppermute(core_part, "core", other_core)

    both = jnp.where(core == 0, jnp.stack([mine, theirs], 1), jnp.stack([theirs, mine], 1))
    both = both.reshape(shards, small.shape[1], width)
    base = jnp.sum(both[:, slots * heads + 2 * slots, 0].astype(jnp.float32))
    own_lens = mine[:, slots * heads + 2 * slots, 0].astype(jnp.int32)
    senders = [(y - dy) % ny * nz + (z - dz) % nz for dy, dz in targets]
    own_lens = jnp.sum(
        jnp.where(jnp.stack(senders)[:, None] == jnp.arange(convs), own_lens[None, :], 0), 1
    )
    index = lax.dynamic_index_in_dim(slot_index, here, 1, keepdims=False)
    index = index.reshape(shards, 2, slots // 2).transpose(1, 0, 2)
    live = index < new_count[here]
    inverse = 1.0 / 500000.0 ** (jnp.arange(0, width, 2, dtype=jnp.float32) / width)
    angles = (base + index.astype(jnp.float32))[..., None] * inverse
    cosine, sine = jnp.cos(angles), jnp.sin(angles)
    q = both[:, : slots * heads].reshape(shards, 2, slots // 2, heads, width)
    q = q.transpose(1, 3, 0, 2, 4).astype(jnp.float32)
    q = rotate(q, cosine[:, None], sine[:, None])
    tokens = shards * slots // 2
    q = q.reshape(2, heads * tokens, width)

    def new_rows(start):
        rows = both[:, start : start + slots].reshape(shards, 2, slots // 2, width)
        return rows.transpose(1, 0, 2, 3)

    new_k = rotate(new_rows(slots * heads).astype(jnp.float32), cosine, sine)
    new_k = new_k.reshape(2 * tokens, width)
    new_v = new_rows(slots * heads + slots).reshape(2 * tokens, width)
    kept = live & (jnp.arange(shards)[None, :, None] % 2 == core)
    key_index = jnp.where(kept, index.astype(jnp.float32), CLOSED).reshape(1, 2 * tokens)
    key_index = jnp.broadcast_to(key_index, (8, 2 * tokens))
    row_index = jnp.broadcast_to(
        index.astype(jnp.float32).reshape(2, 1, tokens, 1), (2, STEP // tokens, tokens, 128)
    ).reshape(2, STEP, 128)

    def plan(which):
        return jnp.concatenate([jnp.full((1,), which, jnp.int32), own_lens])

    start = plan(0)
    sums = attend(1, start, q, [dealt[0, 0]], None, (new_k, new_v, key_index, row_index), 2)
    at_len = 2
    for blocks in arrived[:-2]:
        sums = attend(at_len, start, q, blocks, sums, None, 2)
        at_len += len(blocks)
    ours, others = plan(core), plan(1 - core)
    last_len = at_len + len(arrived[-2])
    message = attend(at_len, others, q, arrived[-2], sums, None, 1)
    message = attend(last_len, others, q, arrived[-1], message, None, 1, "message")
    message = lax.ppermute(message, "core", other_core)
    live_rows = lax.dynamic_index_in_dim(live, core, 0, keepdims=False)
    live_rows = jnp.broadcast_to(live_rows.astype(jnp.float32).reshape(tokens, 1), (tokens, 128))
    sums = attend(at_len, ours, q, arrived[-2], sums, None, 1)
    attended = attend(
        last_len, ours, q, arrived[-1], sums, None, 1, "finish", (message, live_rows)
    )

    attended = attended.reshape(nheads, tokens // nheads, heads * width)
    up = [(i, (i + 1) % nz) for i in range(nz)]
    down = [(i, (i - 1) % nz) for i in range(nz)]
    held = {0: attended}
    for step in range(1, nz // 2):
        held[-step % nz] = lax.ppermute(held[(1 - step) % nz], "z", up)
        held[step] = lax.ppermute(held[step - 1], "z", down)
    first_half, _ = lax.optimization_barrier((weight_y[0], attended))
    second_half, _ = lax.optimization_barrier((weight_y[1], held[2]))
    weight_far = jnp.concatenate([first_half, second_half], 0)
    weight_both = jnp.concatenate(
        [
            lax.ppermute(first_half, "core", other_core),
            lax.ppermute(second_half, "core", other_core),
        ],
        0,
    )
    near = [
        jnp.where(core == 0, out_weight, weight_core),
        jnp.where(core == 0, weight_core, out_weight),
    ]
    far = [
        jnp.where(core == 0, weight_far, weight_both),
        jnp.where(core == 0, weight_both, weight_far),
    ]
    weights = jnp.stack(
        [jnp.where(y == 0, a, b) for a, b in zip(near, far)]
        + [jnp.where(y == 0, b, a) for a, b in zip(near, far)]
    )

    def parts_of(which):
        rows = jnp.stack([held[k] for k in which], 1)
        rows = rows.reshape(-1, heads * width)
        parts = jnp.einsum("rk,wkn->wrn", rows, weights, preferred_element_type=jnp.float32)
        return parts.astype(jnp.bfloat16).reshape(4 * nheads, -1, out_weight.shape[1])

    early = (0, 1, 2, nz - 2, nz - 1)
    late = tuple(range(3, nz - 2))
    early_parts = parts_of(early)
    middle = nz // 2
    from_below, from_above, early_parts = lax.optimization_barrier(
        (held[middle + 1], held[middle - 1], early_parts)
    )
    cut = max(nheads // 2, 1)
    held[middle] = jnp.concatenate(
        [
            lax.ppermute(from_below[:cut], "z", up),
            lax.ppermute(from_above[cut:], "z", down),
        ],
        0,
    )
    parts = jnp.concatenate([early_parts, parts_of(late)], 1)
    got = lax.all_to_all(parts, ("y", "core", "head"), 0, 0, tiled=True)
    got = got.reshape(ny, 2, nheads, nz, tokens // nheads, -1)
    done = jnp.sum(got.astype(jnp.float32), 2).astype(jnp.bfloat16)
    order = early + late
    done = unroll(jnp.stack([done[:, :, order.index(k)] for k in range(nz)], 0), 0, z)
    done = done.reshape(nz, ny, 2, shards // nheads, slots // 2, -1)
    done = done.transpose(3, 1, 0, 2, 4, 5)
    return done.reshape(shards // nheads * convs * slots, -1)


def solution(mesh):
    blk, head = mesh.shape["blk"], mesh.shape["head"]
    fine = Mesh(mesh.devices.reshape(2, blk // 4, 2, head), ("y", "z", "core", "head"))
    blk = ("y", "z", "core")
    return jax.shard_map(
        body,
        mesh=fine,
        in_specs=(
            P(blk, "head", None),
            P(blk, "head", None),
            P(blk, "head", None),
            P(blk, None, "head", None, None),
            P(blk, None, "head", None, None),
            P(blk, None),
            P(),
            P(),
            P("head", blk),
        ),
        out_specs=P("head", blk),
        check_vma=False,
    )
```

```python
import functools

import jax
import jax.numpy as jnp
from jax import lax
from jax.experimental import pallas as pl
from jax.experimental.pallas import tpu as pltpu
from jax.sharding import Mesh, PartitionSpec as P

LOG2_E = 1.4426950408889634
CLOSED = 1.0e9
SHUT = -1.0e30
STEP = 256
LEGS = (
    ((0, 4), (0, 3), (0, -3)),
    ((0, 2), (0, -2), (0, 1), (0, -1)),
    ((1, 4), (1, 3), (1, -3), (1, 2)),
    ((1, -2), (1, 1), (1, -1), (1, 0)),
)


def deal_kernel(targets, at_ref, keys_ref, values_ref, *refs):
    outs, (stage, in_sems, out_sems) = refs[:-3], refs[-3:]
    ny, nz = targets[0]
    slots = keys_ref.shape[3]
    copies = []
    for i, (dy, dz) in enumerate(targets[1]):
        conversation = lax.rem(at_ref[0] + dy, ny) * nz + lax.rem(at_ref[1] + (dz + nz) % nz, nz)
        for j, ref in enumerate((keys_ref, values_ref)):
            copy = pltpu.make_async_copy(
                ref.at[0, conversation, 0], stage.at[i, pl.ds(j * slots, slots)], in_sems.at[i, j]
            )
            copy.start()
            copies.append(copy)
    leaving = []
    for i in range(len(outs)):
        copies[2 * i].wait()
        copies[2 * i + 1].wait()
        copy = pltpu.make_async_copy(stage.at[i], outs[i], out_sems.at[i])
        copy.start()
        leaving.append(copy)
    for copy in leaving:
        copy.wait()


def deal(at, keys, values, grid, targets):
    slots, width = keys.shape[3], keys.shape[4]
    anywhere = pl.BlockSpec(memory_space=pl.ANY)
    count = len(targets)
    return pl.pallas_call(
        functools.partial(deal_kernel, (grid, targets)),
        in_specs=[pl.BlockSpec(memory_space=pltpu.SMEM), anywhere, anywhere],
        out_specs=[anywhere] * count,
        out_shape=[jax.ShapeDtypeStruct((2 * slots, width), jnp.bfloat16)] * count,
        scratch_shapes=[
            pltpu.VMEM((count, 2 * slots, width), jnp.bfloat16),
            pltpu.SemaphoreType.DMA((count, 2)),
            pltpu.SemaphoreType.DMA((count,)),
        ],
    )(at, keys, values)


def attend_kernel(first_len, shards, first, role, plan_ref, q_ref, *refs):
    refs = list(refs)
    keys_ref, values_ref = refs[-2:]
    kv_refs = [refs.pop(0) for _ in range(shards)]
    if first:
        new_k_ref, new_v_ref, key_index_ref, row_index_ref = [refs.pop(0) for _ in range(4)]
    else:
        sums_ref = refs.pop(0)
    if role == "finish":
        message_ref, live_ref = refs.pop(0), refs.pop(0)
    out_ref = refs.pop(0)
    rows, width = q_ref.shape[1], q_ref.shape[2]
    slots = kv_refs[0].shape[0] // 2
    scale = LOG2_E / width**0.5

    @pl.when(pl.program_id(0) == 0)
    def _():
        first_lane = lax.broadcasted_iota(jnp.int32, (slots, width), 1) == 0
        slot = lax.broadcasted_iota(jnp.int32, (slots, width), 0)
        for i, ref in enumerate(kv_refs):
            at = slice(i * slots, (i + 1) * slots)
            keys_ref[at, 0:width] = ref[0:slots, :]
            shut = first_lane & (slot >= plan_ref[first_len + i])
            keys_ref[at, width : 2 * width] = jnp.where(shut, SHUT, 0.0).astype(jnp.bfloat16)
            values_ref[at, 0:width] = ref[slots : 2 * slots, :]
            values_ref[at, width : 2 * width] = jnp.ones((slots, width), jnp.bfloat16)

    lane = lax.broadcasted_iota(jnp.int32, (STEP, width), 1)
    unit = jnp.where(lane == 0, 1.0, 0.0).astype(jnp.bfloat16)
    if first:
        seen = key_index_ref[0:1, :] <= row_index_ref[0]
        ones = jnp.ones((new_v_ref.shape[0], width), jnp.bfloat16)

    if role == "finish":
        row = lax.broadcasted_iota(jnp.int32, (width, 2 * width), 0)
        group = jnp.where(lax.broadcasted_iota(jnp.int32, (width, 2 * width), 1) < width, 0, 3)
        spread = jnp.where((row >= group) & (row < group + 3), 1.0, 0.0).astype(jnp.bfloat16)

    def score(a, b):
        return lax.dot_general(a, b, (((1,), (1,)), ((), ())), preferred_element_type=jnp.float32)

    def scores(step):
        q = q_ref[0, step * STEP : (step + 1) * STEP, :]
        wide = jnp.concatenate([q, unit], 1)
        found = [score(wide, keys_ref[i * slots : (i + 1) * slots, :]) for i in range(shards)]
        if first:
            found.append(jnp.where(seen, score(q, new_k_ref[...]), SHUT))
        return found

    def highest(found, step):
        top = jnp.max(functools.reduce(jnp.maximum, found[:shards]), axis=1, keepdims=True)
        if first:
            return jnp.maximum(top, jnp.max(found[shards], axis=1, keepdims=True))
        before = sums_ref[0, step * STEP : (step + 1) * STEP, 2 * width - 1 : 2 * width]
        return jnp.maximum(top, before)

    steps = rows // STEP
    after = scores(0)
    after_top = highest(after, 0)
    for step in range(steps):
        at = slice(step * STEP, (step + 1) * STEP)
        found, top = after, after_top
        if step + 1 < steps:
            after = scores(step + 1)
        low = top * scale
        if first:
            sums = jnp.zeros((STEP, 2 * width), jnp.float32)
        else:
            sums = sums_ref[0, at, :]
            sums = sums * jnp.exp2(sums[:, 2 * width - 1 : 2 * width] * scale - low)
        for i, s in enumerate(found):
            w = jnp.exp2(s * scale - low).astype(jnp.bfloat16)
            if i < shards:
                v = values_ref[i * slots : (i + 1) * slots, :]
            else:
                v = jnp.concatenate([new_v_ref[...], ones], 1)
            sums = sums + jnp.dot(w, v, preferred_element_type=jnp.float32)
        if step + 1 < steps:
            after_top = highest(after, step + 1)
        if role == "message":
            tail = jnp.zeros((STEP, width), jnp.float32)
            total = sums[:, width : 2 * width]
            for i, value in enumerate((total, jnp.broadcast_to(top, total.shape))):
                for j in range(3):
                    part = value.astype(jnp.bfloat16).astype(jnp.float32)
                    tail = jnp.where(lane == 3 * i + j, part, tail)
                    value = value - part
            out_ref[at, 0:width] = sums[:, 0:width].astype(jnp.bfloat16)
            out_ref[at, width : 2 * width] = tail.astype(jnp.bfloat16)
        elif role == "finish":
            stats = jnp.dot(
                message_ref[at, width : 2 * width], spread, preferred_element_type=jnp.float32
            )
            highest_of_all = jnp.maximum(top, stats[:, width:])
            a = jnp.exp2((top - highest_of_all) * scale)
            b = jnp.exp2((stats[:, width:] - highest_of_all) * scale)
            total = sums[:, width : width + 1] * a + stats[:, :width] * b
            other = message_ref[at, 0:width].astype(jnp.float32)
            mixed = (sums[:, 0:width] * a + other * b) / total
            tokens = live_ref.shape[0]
            for i in range(STEP // tokens):
                head = step * (STEP // tokens) + i
                block = mixed[i * tokens : (i + 1) * tokens, :] * live_ref[...]
                out_ref[:, head * width : (head + 1) * width] = block.astype(jnp.bfloat16)
        else:
            out_ref[0, at, 0:width] = sums[:, 0:width]
            out_ref[0, at, width : 2 * width] = jnp.where(
                lane < width // 2, sums[:, width : 2 * width], top
            )


def attend(first_len, plan, q, kv, sums, new, halves, role="", more=()):
    both, rows, width = q.shape
    slots = kv[0].shape[0] // 2
    part = lambda *tail: pl.BlockSpec((1,) + tail, lambda i, s: (lax.rem(s[0] + i, both), 0, 0))
    whole = lambda a: pl.BlockSpec(a.shape, lambda i, s: (0,) * len(a.shape))
    in_specs = [part(rows, width)] + [whole(a) for a in kv]
    if sums is None:
        in_specs += [whole(a) for a in new[:3]] + [part(*new[3].shape[1:])]
        extra = tuple(new)
    else:
        in_specs.append(whole(sums) if sums.shape[0] == 1 else part(rows, 2 * width))
        extra = (sums,)
    in_specs += [whole(a) for a in more]
    if role == "message":
        out_shape = jax.ShapeDtypeStruct((rows, 2 * width), jnp.bfloat16)
        out_spec = whole(out_shape)
    elif role == "finish":
        tokens = more[1].shape[0]
        out_shape = jax.ShapeDtypeStruct((tokens, rows // tokens * width), jnp.bfloat16)
        out_spec = whole(out_shape)
    else:
        out_shape = jax.ShapeDtypeStruct((halves, rows, 2 * width), jnp.float32)
        out_spec = whole(out_shape) if halves == 1 else part(rows, 2 * width)
    wide = pltpu.VMEM((len(kv) * slots, 2 * width), jnp.bfloat16)
    keys = len(kv) * slots
    return pl.pallas_call(
        functools.partial(attend_kernel, first_len, len(kv), sums is None, role),
        grid_spec=pltpu.PrefetchScalarGridSpec(
            num_scalar_prefetch=1,
            grid=(halves,),
            in_specs=in_specs,
            out_specs=out_spec,
            scratch_shapes=[wide, wide],
        ),
        out_shape=out_shape,
        compiler_params=pltpu.CompilerParams(vmem_limit_bytes=40 * 1024 * 1024),
        cost_estimate=pl.CostEstimate(
            flops=16 * halves * rows * width * keys,
            bytes_accessed=halves * rows * width * 16,
            transcendentals=halves * rows * keys,
        ),
    )(plan, q, *kv, *extra, *more)


def rotate(values, cosine, sine):
    half = values.shape[-1] // 2
    first, second = values[..., :half], values[..., half:]
    return jnp.concatenate(
        [first * cosine - second * sine, second * cosine + first * sine], -1
    ).astype(jnp.bfloat16)


def body(
    queries,
    unrotated_key_rows,
    incoming_value_rows,
    cache_keys,
    stored_value_rows,
    cache_len,
    new_count,
    slot_index,
    out_weight,
):
    ny, nz, nheads = lax.axis_size("y"), lax.axis_size("z"), lax.axis_size("head")
    y, z, core = lax.axis_index("y"), lax.axis_index("z"), lax.axis_index("core")
    convs, slots = slot_index.shape[1], slot_index.shape[2]
    shards = slot_index.shape[0]
    heads, width = queries.shape[1], queries.shape[2]
    here = y * nz + z
    other_core = [(0, 1), (1, 0)]

    def unroll(values, axis, by):
        size = values.shape[axis]
        twice = jnp.concatenate([values, values], axis)
        return lax.dynamic_slice_in_dim(twice, (size - by) % size, size, axis)

    small = jnp.concatenate(
        [
            queries.reshape(convs, slots * heads, width),
            unrotated_key_rows.reshape(convs, slots, width),
            incoming_value_rows.reshape(convs, slots, width),
            jnp.broadcast_to(
                cache_len[0].astype(jnp.bfloat16)[:, None, None], (convs, 16 - 2 * slots, width)
            ),
        ],
        1,
    )
    mine = lax.all_to_all(small, ("y", "z"), 0, 0, tiled=True)
    theirs = lax.ppermute(mine, "core", other_core)

    targets = ((0, 0),) + tuple(leg for group in LEGS for leg in group)
    at = jnp.stack([y, z]).astype(jnp.int32)
    dealt = dict(zip(targets, deal(at, cache_keys, stored_value_rows, (ny, nz), targets)))

    def sent(dy, dz):
        route = [
            (a * nz + b, (a + dy) % ny * nz + (b + dz) % nz) for a in range(ny) for b in range(nz)
        ]
        return lax.ppermute(dealt[dy, dz], ("y", "z"), route)

    depth = out_weight.shape[0] * 3 // 8
    other_y = [(0, 1), (1, 0)]
    weight_y = [lax.ppermute(out_weight[:depth], "y", other_y)]
    arrived = []
    for i, group in enumerate(LEGS):
        if i == 1:
            late_legs = [leg for some in LEGS[1:] for leg in some]
            held_back = lax.optimization_barrier(
                tuple(dealt[leg] for leg in late_legs) + (weight_y[0],)
            )
            weight_y[0] = held_back[-1]
            dealt.update(zip(late_legs, held_back))
        arrived.append([sent(*leg) for leg in group])
    rest, _ = lax.optimization_barrier((out_weight[depth:], arrived[-1][-1]))
    weight_y.append(lax.ppermute(rest, "y", other_y))
    core_part, _ = lax.optimization_barrier((out_weight, arrived[0][0]))
    weight_core = lax.ppermute(core_part, "core", other_core)

    both = jnp.where(core == 0, jnp.stack([mine, theirs], 1), jnp.stack([theirs, mine], 1))
    both = both.reshape(shards, small.shape[1], width)
    base = jnp.sum(both[:, slots * heads + 2 * slots, 0].astype(jnp.float32))
    own_lens = mine[:, slots * heads + 2 * slots, 0].astype(jnp.int32)
    senders = [(y - dy) % ny * nz + (z - dz) % nz for dy, dz in targets]
    own_lens = jnp.sum(
        jnp.where(jnp.stack(senders)[:, None] == jnp.arange(convs), own_lens[None, :], 0), 1
    )
    index = lax.dynamic_index_in_dim(slot_index, here, 1, keepdims=False)
    index = index.reshape(shards, 2, slots // 2).transpose(1, 0, 2)
    live = index < new_count[here]
    inverse = 1.0 / 500000.0 ** (jnp.arange(0, width, 2, dtype=jnp.float32) / width)
    angles = (base + index.astype(jnp.float32))[..., None] * inverse
    cosine, sine = jnp.cos(angles), jnp.sin(angles)
    q = both[:, : slots * heads].reshape(shards, 2, slots // 2, heads, width)
    q = q.transpose(1, 3, 0, 2, 4).astype(jnp.float32)
    q = rotate(q, cosine[:, None], sine[:, None])
    tokens = shards * slots // 2
    q = q.reshape(2, heads * tokens, width)

    def new_rows(start):
        rows = both[:, start : start + slots].reshape(shards, 2, slots // 2, width)
        return rows.transpose(1, 0, 2, 3)

    new_k = rotate(new_rows(slots * heads).astype(jnp.float32), cosine, sine)
    new_k = new_k.reshape(2 * tokens, width)
    new_v = new_rows(slots * heads + slots).reshape(2 * tokens, width)
    kept = live & (jnp.arange(shards)[None, :, None] % 2 == core)
    key_index = jnp.where(kept, index.astype(jnp.float32), CLOSED).reshape(1, 2 * tokens)
    key_index = jnp.broadcast_to(key_index, (8, 2 * tokens))
    row_index = jnp.broadcast_to(
        index.astype(jnp.float32).reshape(2, 1, tokens, 1), (2, STEP // tokens, tokens, 128)
    ).reshape(2, STEP, 128)

    def plan(which):
        return jnp.concatenate([jnp.full((1,), which, jnp.int32), own_lens])

    start = plan(0)
    sums = attend(1, start, q, [dealt[0, 0]], None, (new_k, new_v, key_index, row_index), 2)
    at_len = 2
    for blocks in arrived[:-2]:
        sums = attend(at_len, start, q, blocks, sums, None, 2)
        at_len += len(blocks)
    ours, others = plan(core), plan(1 - core)
    last_len = at_len + len(arrived[-2])
    message = attend(at_len, others, q, arrived[-2], sums, None, 1)
    message = attend(last_len, others, q, arrived[-1], message, None, 1, "message")
    message = lax.ppermute(message, "core", other_core)
    live_rows = lax.dynamic_index_in_dim(live, core, 0, keepdims=False)
    live_rows = jnp.broadcast_to(live_rows.astype(jnp.float32).reshape(tokens, 1), (tokens, 128))
    sums = attend(at_len, ours, q, arrived[-2], sums, None, 1)
    attended = attend(
        last_len, ours, q, arrived[-1], sums, None, 1, "finish", (message, live_rows)
    )

    attended = attended.reshape(nheads, tokens // nheads, heads * width)
    up = [(i, (i + 1) % nz) for i in range(nz)]
    down = [(i, (i - 1) % nz) for i in range(nz)]
    held = {0: attended}
    for step in range(1, nz // 2):
        held[-step % nz] = lax.ppermute(held[(1 - step) % nz], "z", up)
        held[step] = lax.ppermute(held[step - 1], "z", down)
    first_half, _ = lax.optimization_barrier((weight_y[0], attended))
    second_half, _ = lax.optimization_barrier((weight_y[1], held[2]))
    weight_far = jnp.concatenate([first_half, second_half], 0)
    weight_both = jnp.concatenate(
        [
            lax.ppermute(first_half, "core", other_core),
            lax.ppermute(second_half, "core", other_core),
        ],
        0,
    )
    near = [
        jnp.where(core == 0, out_weight, weight_core),
        jnp.where(core == 0, weight_core, out_weight),
    ]
    far = [
        jnp.where(core == 0, weight_far, weight_both),
        jnp.where(core == 0, weight_both, weight_far),
    ]
    weights = jnp.stack(
        [jnp.where(y == 0, a, b) for a, b in zip(near, far)]
        + [jnp.where(y == 0, b, a) for a, b in zip(near, far)]
    )

    def parts_of(which):
        rows = jnp.stack([held[k] for k in which], 1)
        rows = rows.reshape(-1, heads * width)
        parts = jnp.einsum("rk,wkn->wrn", rows, weights, preferred_element_type=jnp.float32)
        return parts.astype(jnp.bfloat16).reshape(4 * nheads, -1, out_weight.shape[1])

    early = (0, 1, 2, nz - 2, nz - 1)
    late = tuple(range(3, nz - 2))
    early_parts = parts_of(early)
    middle = nz // 2
    from_below, from_above, early_parts = lax.optimization_barrier(
        (held[middle + 1], held[middle - 1], early_parts)
    )
    cut = max(nheads // 2, 1)
    held[middle] = jnp.concatenate(
        [
            lax.ppermute(from_below[:cut], "z", up),
            lax.ppermute(from_above[cut:], "z", down),
        ],
        0,
    )
    parts = jnp.concatenate([early_parts, parts_of(late)], 1)
    got = lax.all_to_all(parts, ("y", "core", "head"), 0, 0, tiled=True)
    got = got.reshape(ny, 2, nheads, nz, tokens // nheads, -1)
    done = jnp.sum(got.astype(jnp.float32), 2).astype(jnp.bfloat16)
    order = early + late
    done = unroll(jnp.stack([done[:, :, order.index(k)] for k in range(nz)], 0), 0, z)
    done = done.reshape(nz, ny, 2, shards // nheads, slots // 2, -1)
    done = done.transpose(3, 1, 0, 2, 4, 5)
    return done.reshape(shards // nheads * convs * slots, -1)


def solution(mesh):
    blk, head = mesh.shape["blk"], mesh.shape["head"]
    fine = Mesh(mesh.devices.reshape(2, blk // 4, 2, head), ("y", "z", "core", "head"))
    blk = ("y", "z", "core")
    return jax.shard_map(
        body,
        mesh=fine,
        in_specs=(
            P(blk, "head", None),
            P(blk, "head", None),
            P(blk, "head", None),
            P(blk, None, "head", None, None),
            P(blk, None, "head", None, None),
            P(blk, None),
            P(),
            P(),
            P("head", blk),
        ),
        out_specs=P("head", blk),
        check_vma=False,
    )
```
